256 devices in a mesh: dp: 64 (over z, x, core), group: 4 (over y).
Axes of the slice: x: 4, y: 4, z: 8, core: 2. Of those that a mesh axis runs over, the one named last changes fastest.
Arguments:
- frames: bfloat16 [64, 4, 384, 8192], P('dp', 'group'), may hold values from -6 to 6
- lengths: int32 [64, 4, 4], P('dp', 'group'), may hold values from 32 to 96, as said below
- probes: bfloat16 [8192, 256], P('dp'), may hold values from -0.0625 to 0.0625
Outputs:
- basis: float32 [8192, 256], P('dp')
- factor: float32 [256, 256], replicated
The draws below stay inside these ranges and needn't reach their ends.
Inputs may be any that keep to these rules, and one draw needn't show every extreme that they name: `lengths`: each device's spans lie back to back from its first frame slot; the device at index 0 of both axes has all 4 spans of length 96.
All inputs are finite; a program needn't handle non-finite values.
Results may differ from the reference program's by a relative error of at most 0.0031.
Values may be sent and summed in bfloat16 or wider, within the bound.
A program may use at most 128 MiB of HBM per device.

```python
import math
import jax
import jax.numpy as jnp
from jax import lax

D = 8192
K = 256
FR = 384
CH = 4
LMAX = 96
LMIN = 32
N_DP = 64
N_GROUP = 4


def draw_lengths(key, part):
    values = jax.random.randint(key, (N_DP, N_GROUP, CH), LMIN, LMAX + 1, dtype=jnp.int32)
    return values.at[0, 0, :].set(LMAX)


def shard_levels(rng, shape, pieces, least, largest):
    level, own = 1.0, jax.random.fold_in(rng, 6)
    for axis_at, shards_of in pieces:
        draws = jnp.exp(jax.random.uniform(jax.random.fold_in(own, axis_at), (shards_of,), jnp.float32, least / len(pieces), largest / len(pieces)))
        level = level * jnp.repeat(draws, shape[axis_at] // shards_of).reshape([-1 if axis == axis_at else 1 for axis in range(len(shape))])
    return level


def gaussian(key, shape, width, bound, cuts=(), held_as=jnp.bfloat16):
    array = width * jax.random.normal(key, shape, jnp.float32)
    if cuts:
        array = array * shard_levels(key, shape, cuts, -0.22, 0.18)
    return jnp.clip(array, -bound, bound).astype(held_as)


def setup_inputs(seed: int = 0) -> dict:
    key_of = jax.random.split(jax.random.key(seed), 4)
    frames = gaussian(key_of[0], (N_DP, N_GROUP, FR, D), 1.0, 6.0, ((0, 64), (1, 4)))
    lengths = draw_lengths(jax.random.fold_in(key_of[3], 71), 0)
    probes = gaussian(key_of[2], (D, K), D ** -0.5, 0.0625, ((0, 64),))
    return {"frames": frames, "lengths": lengths, "probes": probes}


def pair_mask(lengths, count):
    ends = jnp.cumsum(lengths).astype(jnp.int32)
    starts = ends - lengths
    position = jnp.arange(count, dtype=jnp.int32)
    inside = (position[:, None] >= starts[None, :] + 1) & (position[:, None] <= ends[None, :] - 1)
    return jnp.any(inside, axis=1)

def reference(frames, lengths, probes):
    scale = 1.0 / math.sqrt(D * FR * N_DP * N_GROUP)
    all_frames = frames.reshape(N_DP * N_GROUP, FR, D)
    all_lengths = lengths.reshape(N_DP * N_GROUP, CH)

    def accumulate(total, item):
        block, sizes = item
        projected = jnp.dot(block.astype(jnp.float32), probes.astype(jnp.float32), preferred_element_type=jnp.float32).astype(jnp.bfloat16)
        shifted = jnp.concatenate([jnp.zeros((1, K), jnp.bfloat16), projected[:-1]], axis=0)
        paired = jnp.where(pair_mask(sizes, FR)[:, None], shifted, jnp.zeros_like(shifted)).astype(jnp.bfloat16)
        term = jnp.dot(block.T.astype(jnp.float32), paired.astype(jnp.float32), preferred_element_type=jnp.float32)
        return (total + scale * term, None)
    sketch, _ = lax.scan(accumulate, jnp.zeros((D, K), jnp.float32), (all_frames, all_lengths))
    gram = jnp.dot(sketch.T, sketch, precision=lax.Precision.HIGHEST)
    lower = jnp.linalg.cholesky(gram)
    basis = jax.scipy.linalg.solve_triangular(lower, sketch.T, lower=True).T * math.sqrt(D)
    return (basis, lower.T)
```

```python
import functools
import math

import jax
import jax.numpy as jnp
from jax import lax
from jax.experimental import pallas as pl
from jax.experimental.pallas import tpu as pltpu
from jax.sharding import PartitionSpec as P

MESH = pl.DeviceIdType.MESH
NZ, NX, NY, NC = 8, 4, 4, 2
NXY = NX * NY
NXYC = NXY * NC
BLOCK = 128
PIECE = BLOCK // NY


def device(z, x, c, y):
    return ((z * NX + x) * NC + c, y)


def remote(src, dst, send, recv, where):
    return pltpu.make_async_remote_copy(
        src_ref=src,
        dst_ref=dst,
        send_sem=send,
        recv_sem=recv,
        device_id=where,
        device_id_type=MESH,
    )


def kernel(
    scale,
    lens,
    frames,
    probes,
    sketch_ref,
    gram_ref,
    w,
    wt,
    pb,
    masks,
    part,
    other,
    paired,
    tsend,
    trecv,
    rows,
    zrecv,
    local_sem,
    probe_sem,
    frame_sems,
    mask_sems,
    part_sems,
    az_s,
    az_r,
    ap_s,
    ap_r,
    rs_s,
    rs_r,
    rz_s,
    rz_r,
    y_s,
    y_r,
    gsend,
    grecv,
    gz,
    g_s,
    g_r,
    gz_s,
    gz_r,
    ga_s,
    ga_r,
):
    dp = lax.axis_index("dp")
    y = lax.axis_index("group")
    c = dp % NC
    x = (dp // NC) % NX
    z = dp // (NC * NX)
    count = frames.shape[0]

    def at_z(k):
        return device((z + k) % NZ, x, c, y)

    def at_xy(k):
        return (x + k // NY) % NX, (y + k % NY) % NY

    def dev_xy(k):
        px, py = at_xy(k)
        return device(z, px, c, py)

    def at_xyc(k):
        return (x + k // (NY * NC)) % NX, (y + (k // NC) % NY) % NY, (c + k % NC) % NC

    def dev_xyc(k):
        px, py, pc = at_xyc(k)
        return device(z, px, pc, py)

    partner = device(z, x, 1 - c, y)

    def own(i, _):
        col = ((i % NZ) * NX + i // NZ) * NC + c
        pltpu.make_async_copy(
            frames.at[:, pl.ds(pl.multiple_of(col * BLOCK, BLOCK), BLOCK)],
            w.at[pl.ds(pl.multiple_of(c * count, 128), count), pl.ds(pl.multiple_of(i * BLOCK, BLOCK), BLOCK)],
            local_sem,
        ).start()
        return 0

    mine = pltpu.make_async_copy(
        probes.at[pl.ds(pl.multiple_of(y * PIECE, PIECE), PIECE)], pb.at[x, z, y], probe_sem
    )
    mine.start()
    lax.fori_loop(0, NZ * NX, own, 0)

    barrier = pltpu.get_barrier_semaphore()

    def greet_z(k, _):
        pl.semaphore_signal(barrier, inc=1, device_id=at_z(k), device_id_type=MESH)
        return 0

    def greet_xyc(k, _):
        pl.semaphore_signal(barrier, inc=1, device_id=dev_xyc(k), device_id_type=MESH)
        return 0

    lax.fori_loop(1, NZ, greet_z, 0)
    lax.fori_loop(1, NXYC, greet_xyc, 0)

    position = lax.broadcasted_iota(jnp.int32, (count, BLOCK), 0)
    inside = jnp.zeros((count, BLOCK), jnp.float32)
    start = jnp.int32(0)
    for span in range(4):
        end = start + lens[0, 0, span]
        inside = inside + jnp.where(
            jnp.logical_and(position >= start + 1, position <= end - 1), 1.0, 0.0
        )
        start = end
    masks[c] = inside

    pl.semaphore_wait(barrier, NZ - 1 + NXYC - 1)

    mine.wait()

    def gather_z(k):
        return remote(pb.at[x, z, y], pb.at[x, z, y], az_s.at[k], az_r.at[k], at_z(k))

    def start_gather_z(k, _):
        gather_z(k).start()
        return 0

    lax.fori_loop(1, NZ, start_gather_z, 0)

    def give(i, _):
        col = ((i % NZ) * NX + i // NZ) * NC + (1 - c)
        remote(
            frames.at[:, pl.ds(pl.multiple_of(col * BLOCK, BLOCK), BLOCK)],
            w.at[pl.ds(pl.multiple_of(c * count, 128), count), pl.ds(pl.multiple_of(i * BLOCK, BLOCK), BLOCK)],
            frame_sems.at[0],
            frame_sems.at[1],
            partner,
        ).start()
        return 0

    lax.fori_loop(0, NZ * NX, give, 0)
    mask_copy = remote(masks.at[c], masks.at[c], mask_sems.at[0], mask_sems.at[1], partner)
    mask_copy.start()

    def wait_gather_z(k, _):
        gather_z(k).wait()
        return 0

    lax.fori_loop(1, NZ, wait_gather_z, 0)

    def gather_xy(k):
        return remote(pb.at[x, :, y], pb.at[x, :, y], ap_s.at[k], ap_r.at[k], dev_xy(k))

    def start_gather_xy(k, _):
        gather_xy(k).start()
        return 0

    lax.fori_loop(1, NXY, start_gather_xy, 0)

    mine_rows = w.at[pl.ds(pl.multiple_of(c * count, 128), count)]
    pltpu.make_async_copy(mine_rows, mine_rows, local_sem).wait()
    frames_copy = remote(mine_rows, mine_rows, frame_sems.at[0], frame_sems.at[1], partner)
    frames_copy.wait()
    mask_copy.wait()

    def turn(i, _):
        block = w[:, pl.ds(pl.multiple_of(i * BLOCK, BLOCK), BLOCK)]
        wt[i // NZ, i % NZ] = block.T.reshape(NY, PIECE, 2 * count)
        return 0

    lax.fori_loop(0, NZ * NX, turn, 0)

    def project(dx, _):
        def arrived(dy, _):
            gather_xy(dx * NY + dy).wait_recv()
            return 0

        lax.fori_loop(jnp.where(dx == 0, 1, 0), NY, arrived, 0)
        px = (x - dx + NX) % NX
        depth = NZ * BLOCK
        block = pb[px].reshape(depth, pb.shape[-1])
        product = jnp.dot(
            w[:, pl.ds(pl.multiple_of(px * depth, depth), depth)],
            block,
            preferred_element_type=jnp.float32,
        )

        @pl.when(dx == 0)
        def _():
            part[...] = product

        @pl.when(dx > 0)
        def _():
            part[...] += product

        return 0

    lax.fori_loop(0, NX, project, 0)

    swap = remote(part, other, part_sems.at[0], part_sems.at[1], partner)
    swap.start()
    swap.wait()
    shifted = pltpu.roll(part[...] + other[...], 1, 0)
    mask = masks[...].reshape(2 * count, BLOCK)
    mask = jnp.concatenate([mask, mask], axis=1)
    paired[...] = jnp.where(mask > 0.5, shifted, 0.0).astype(jnp.bfloat16)

    def term(px, py):
        lhs = wt[px, :, py].reshape(NZ * PIECE, 2 * count)
        return jnp.dot(lhs, paired[...], preferred_element_type=jnp.float32)

    def scatter_xy(k):
        return remote(tsend.at[k], trecv.at[k], rs_s.at[k], rs_r.at[k], dev_xy(k))

    def start_scatter_xy(k, _):
        px, py = at_xy(k)
        tsend[k] = term(px, py).astype(jnp.bfloat16)
        scatter_xy(k).start()
        return 0

    lax.fori_loop(1, NXY, start_scatter_xy, 0)
    rows[...] = term(x, y)

    def sum_xy(k, _):
        scatter_xy(k).wait_recv()
        rows[...] += trecv[k].astype(jnp.float32)
        return 0

    lax.fori_loop(1, NXY, sum_xy, 0)

    def scatter_z(k):
        there = (z + k) % NZ
        return remote(
            rows.at[pl.ds(pl.multiple_of(there * PIECE, PIECE), PIECE)],
            zrecv.at[k],
            rz_s.at[k],
            rz_r.at[k],
            at_z(k),
        )

    def start_scatter_z(k, _):
        scatter_z(k).start()
        return 0

    lax.fori_loop(1, NZ, start_scatter_z, 0)
    total = rows[pl.ds(pl.multiple_of(z * PIECE, PIECE), PIECE)]

    def sum_z(k, total):
        scatter_z(k).wait_recv()
        return total + zrecv[k]

    total = lax.fori_loop(1, NZ, sum_z, total) * scale
    here = pl.ds(pl.multiple_of(y * PIECE, PIECE), PIECE)
    sketch_ref[here] = total

    def gather_y(k):
        return remote(
            sketch_ref.at[here],
            sketch_ref.at[here],
            y_s.at[k],
            y_r.at[k],
            device(z, x, c, (y + k) % NY),
        )

    gsend[...] = jnp.dot(
        total.T, total, preferred_element_type=jnp.float32, precision=lax.Precision.HIGHEST
    ).reshape(gsend.shape)

    def scatter_g(k):
        px, py, pc = at_xyc(k)
        return remote(
            gsend.at[(px * NY + py) * NC + pc], grecv.at[k], g_s.at[k], g_r.at[k], dev_xyc(k)
        )

    def start_scatter_g(k, _):
        scatter_g(k).start()
        return 0

    lax.fori_loop(1, NXYC, start_scatter_g, 0)

    def start_gather_y(k, _):
        gather_y(k).start()
        return 0

    lax.fori_loop(1, NY, start_gather_y, 0)
    me = (x * NY + y) * NC + c

    def sum_g(k, acc):
        scatter_g(k).wait_recv()
        return acc + grecv[k]

    gz[z] = lax.fori_loop(1, NXYC, sum_g, gsend[me])

    def spread_z(k):
        return remote(gz.at[z], gz.at[z], gz_s.at[k], gz_r.at[k], at_z(k))

    def start_spread_z(k, _):
        spread_z(k).start()
        return 0

    def wait_spread_z(k, _):
        spread_z(k).wait()
        return 0

    lax.fori_loop(1, NZ, start_spread_z, 0)
    lax.fori_loop(1, NZ, wait_spread_z, 0)
    acc = gz[0]
    for k in range(1, NZ):
        acc = acc + gz[k]
    gram_ref[me] = acc

    def gather_g(k):
        return remote(gram_ref.at[me], gram_ref.at[me], ga_s.at[k], ga_r.at[k], dev_xyc(k))

    def start_gather_g(k, _):
        gather_g(k).start()
        return 0

    def wait_gather_g(k, _):
        gather_g(k).wait()
        return 0

    lax.fori_loop(1, NXYC, start_gather_g, 0)

    def end_xy(k, _):
        gather_xy(k).wait_send()
        scatter_xy(k).wait_send()
        return 0

    def end_z(k, _):
        scatter_z(k).wait_send()
        return 0

    def end_g(k, _):
        scatter_g(k).wait_send()
        return 0

    def end_y(k, _):
        gather_y(k).wait()
        return 0

    lax.fori_loop(1, NXY, end_xy, 0)
    lax.fori_loop(1, NZ, end_z, 0)
    lax.fori_loop(1, NXYC, end_g, 0)
    lax.fori_loop(1, NY, end_y, 0)
    lax.fori_loop(1, NXYC, wait_gather_g, 0)


def sketch_and_gram(frames, lengths, probes, devices):
    count, width = frames.shape
    columns = probes.shape[1]
    scale = 1.0 / math.sqrt(width * count * devices)
    half = width // NC
    dma = pltpu.SemaphoreType.DMA
    f32, bf16 = jnp.float32, jnp.bfloat16
    return pl.pallas_call(
        functools.partial(kernel, scale),
        out_shape=(
            jax.ShapeDtypeStruct((BLOCK, columns), f32),
            jax.ShapeDtypeStruct((NXYC, columns // NXYC, columns), f32),
        ),
        in_specs=[
            pl.BlockSpec(memory_space=pltpu.SMEM),
            pl.BlockSpec(memory_space=pl.ANY),
            pl.BlockSpec(memory_space=pl.ANY),
        ],
        out_specs=(pl.BlockSpec(memory_space=pltpu.VMEM), pl.BlockSpec(memory_space=pltpu.VMEM)),
        scratch_shapes=[
            pltpu.VMEM((NC * count, half), bf16),
            pltpu.VMEM((NX, NZ, NY, PIECE, NC * count), bf16),
            pltpu.VMEM((NX, NZ, NY, PIECE, columns), bf16),
            pltpu.VMEM((NC, count, BLOCK), f32),
            pltpu.VMEM((NC * count, columns), f32),
            pltpu.VMEM((NC * count, columns), f32),
            pltpu.VMEM((NC * count, columns), bf16),
            pltpu.VMEM((NXY, NZ * PIECE, columns), bf16),
            pltpu.VMEM((NXY, NZ * PIECE, columns), bf16),
            pltpu.VMEM((NZ * PIECE, columns), f32),
            pltpu.VMEM((NZ, PIECE, columns), f32),
            dma,
            dma,
            dma((2,)),
            dma((2,)),
            dma((2,)),
            dma((NZ,)),
            dma((NZ,)),
            dma((NXY,)),
            dma((NXY,)),
            dma((NXY,)),
            dma((NXY,)),
            dma((NZ,)),
            dma((NZ,)),
            dma((NY,)),
            dma((NY,)),
            pltpu.VMEM((NXYC, columns // NXYC, columns), f32),
            pltpu.VMEM((NXYC, columns // NXYC, columns), f32),
            pltpu.VMEM((NZ, columns // NXYC, columns), f32),
            dma((NXYC,)),
            dma((NXYC,)),
            dma((NZ,)),
            dma((NZ,)),
            dma((NXYC,)),
            dma((NXYC,)),
        ],
        compiler_params=pltpu.CompilerParams(
            collective_id=0, has_side_effects=True, vmem_limit_bytes=48 << 20
        ),
    )(lengths, frames, probes)


def shards(frames, lengths, probes):
    local = frames.reshape(frames.shape[2], frames.shape[3])
    width = local.shape[1]
    columns = probes.shape[1]
    devices = lax.axis_size("dp") * lax.axis_size("group")
    sketch, gram = sketch_and_gram(local, lengths, probes, devices)
    gram = gram.reshape(columns, columns)
    lower = jnp.linalg.cholesky(gram)
    basis = jax.scipy.linalg.solve_triangular(lower, sketch.T, lower=True).T * math.sqrt(width)
    return (basis, lower.T)


def solution(mesh):
    placed = (P("dp", "group", None, None), P("dp", "group", None), P("dp", None))
    return jax.shard_map(
        shards, mesh=mesh, in_specs=placed, out_specs=(P("dp", None), P()), check_vma=False
    )
```

```python
import functools
import math

import jax
import jax.numpy as jnp
from jax import lax
from jax.experimental import pallas as pl
from jax.experimental.pallas import tpu as pltpu
from jax.sharding import PartitionSpec as P

MESH = pl.DeviceIdType.MESH
NZ, NX, NY, NC = 8, 4, 4, 2
NXY = NX * NY
NXYC = NXY * NC
BLOCK = 128
PIECE = BLOCK // NY


def device(z, x, c, y):
    return ((z * NX + x) * NC + c, y)


def remote(src, dst, send, recv, where):
    return pltpu.make_async_remote_copy(
        src_ref=src,
        dst_ref=dst,
        send_sem=send,
        recv_sem=recv,
        device_id=where,
        device_id_type=MESH,
    )


def kernel(
    scale,
    lens,
    frames,
    probes,
    sketch_ref,
    gram_ref,
    w,
    wt,
    pb,
    masks,
    part,
    other,
    paired,
    tsend,
    trecv,
    rows,
    zrecv,
    local_sem,
    probe_sem,
    frame_sems,
    mask_sems,
    part_sems,
    az_s,
    az_r,
    ap_s,
    ap_r,
    rs_s,
    rs_r,
    rz_s,
    rz_r,
    y_s,
    y_r,
    gsend,
    grecv,
    gz,
    g_s,
    g_r,
    gz_s,
    gz_r,
    ga_s,
    ga_r,
):
    dp = lax.axis_index("dp")
    y = lax.axis_index("group")
    c = dp % NC
    x = (dp // NC) % NX
    z = dp // (NC * NX)
    count = frames.shape[0]

    def at_z(k):
        return device((z + k) % NZ, x, c, y)

    def at_xy(k):
        return (x + k // NY) % NX, (y + k % NY) % NY

    def dev_xy(k):
        px, py = at_xy(k)
        return device(z, px, c, py)

    def at_xyc(k):
        return (x + k // (NY * NC)) % NX, (y + (k // NC) % NY) % NY, (c + k % NC) % NC

    def dev_xyc(k):
        px, py, pc = at_xyc(k)
        return device(z, px, pc, py)

    partner = device(z, x, 1 - c, y)

    def own(i, _):
        col = ((i % NZ) * NX + i // NZ) * NC + c
        pltpu.make_async_copy(
            frames.at[:, pl.ds(pl.multiple_of(col * BLOCK, BLOCK), BLOCK)],
            w.at[pl.ds(pl.multiple_of(c * count, 128), count), pl.ds(pl.multiple_of(i * BLOCK, BLOCK), BLOCK)],
            local_sem,
        ).start()
        return 0

    mine = pltpu.make_async_copy(
        probes.at[pl.ds(pl.multiple_of(y * PIECE, PIECE), PIECE)], pb.at[x, z, y], probe_sem
    )
    mine.start()
    lax.fori_loop(0, NZ * NX, own, 0)

    barrier = pltpu.get_barrier_semaphore()

    def greet_z(k, _):
        pl.semaphore_signal(barrier, inc=1, device_id=at_z(k), device_id_type=MESH)
        return 0

    def greet_xyc(k, _):
        pl.semaphore_signal(barrier, inc=1, device_id=dev_xyc(k), device_id_type=MESH)
        return 0

    lax.fori_loop(1, NZ, greet_z, 0)
    lax.fori_loop(1, NXYC, greet_xyc, 0)

    position = lax.broadcasted_iota(jnp.int32, (count, BLOCK), 0)
    inside = jnp.zeros((count, BLOCK), jnp.float32)
    start = jnp.int32(0)
    for span in range(4):
        end = start + lens[0, 0, span]
        inside = inside + jnp.where(
            jnp.logical_and(position >= start + 1, position <= end - 1), 1.0, 0.0
        )
        start = end
    masks[c] = inside

    pl.semaphore_wait(barrier, NZ - 1 + NXYC - 1)

    mine.wait()

    def gather_z(k):
        return remote(pb.at[x, z, y], pb.at[x, z, y], az_s.at[k], az_r.at[k], at_z(k))

    def start_gather_z(k, _):
        gather_z(k).start()
        return 0

    lax.fori_loop(1, NZ, start_gather_z, 0)

    def give(i, _):
        col = ((i % NZ) * NX + i // NZ) * NC + (1 - c)
        remote(
            frames.at[:, pl.ds(pl.multiple_of(col * BLOCK, BLOCK), BLOCK)],
            w.at[pl.ds(pl.multiple_of(c * count, 128), count), pl.ds(pl.multiple_of(i * BLOCK, BLOCK), BLOCK)],
            frame_sems.at[0],
            frame_sems.at[1],
            partner,
        ).start()
        return 0

    lax.fori_loop(0, NZ * NX, give, 0)
    mask_copy = remote(masks.at[c], masks.at[c], mask_sems.at[0], mask_sems.at[1], partner)
    mask_copy.start()

    def wait_gather_z(k, _):
        gather_z(k).wait()
        return 0

    lax.fori_loop(1, NZ, wait_gather_z, 0)

    def gather_xy(k):
        return remote(pb.at[x, :, y], pb.at[x, :, y], ap_s.at[k], ap_r.at[k], dev_xy(k))

    def start_gather_xy(k, _):
        gather_xy(k).start()
        return 0

    lax.fori_loop(1, NXY, start_gather_xy, 0)

    mine_rows = w.at[pl.ds(pl.multiple_of(c * count, 128), count)]
    pltpu.make_async_copy(mine_rows, mine_rows, local_sem).wait()
    frames_copy = remote(mine_rows, mine_rows, frame_sems.at[0], frame_sems.at[1], partner)
    frames_copy.wait()
    mask_copy.wait()

    def turn(i, _):
        block = w[:, pl.ds(pl.multiple_of(i * BLOCK, BLOCK), BLOCK)]
        wt[i // NZ, i % NZ] = block.T.reshape(NY, PIECE, 2 * count)
        return 0

    lax.fori_loop(0, NZ * NX, turn, 0)

    def project(dx, _):
        def arrived(dy, _):
            gather_xy(dx * NY + dy).wait_recv()
            return 0

        lax.fori_loop(jnp.where(dx == 0, 1, 0), NY, arrived, 0)
        px = (x - dx + NX) % NX
        depth = NZ * BLOCK
        block = pb[px].reshape(depth, pb.shape[-1])
        product = jnp.dot(
            w[:, pl.ds(pl.multiple_of(px * depth, depth), depth)],
            block,
            preferred_element_type=jnp.float32,
        )

        @pl.when(dx == 0)
        def _():
            part[...] = product

        @pl.when(dx > 0)
        def _():
            part[...] += product

        return 0

    lax.fori_loop(0, NX, project, 0)

    swap = remote(part, other, part_sems.at[0], part_sems.at[1], partner)
    swap.start()
    swap.wait()
    shifted = pltpu.roll(part[...] + other[...], 1, 0)
    mask = masks[...].reshape(2 * count, BLOCK)
    mask = jnp.concatenate([mask, mask], axis=1)
    paired[...] = jnp.where(mask > 0.5, shifted, 0.0).astype(jnp.bfloat16)

    def term(px, py):
        lhs = wt[px, :, py].reshape(NZ * PIECE, 2 * count)
        return jnp.dot(lhs, paired[...], preferred_element_type=jnp.float32)

    def scatter_xy(k):
        return remote(tsend.at[k], trecv.at[k], rs_s.at[k], rs_r.at[k], dev_xy(k))

    def start_scatter_xy(k, _):
        px, py = at_xy(k)
        tsend[k] = term(px, py).astype(jnp.bfloat16)
        scatter_xy(k).start()
        return 0

    lax.fori_loop(1, NXY, start_scatter_xy, 0)
    rows[...] = term(x, y)

    def sum_xy(k, _):
        scatter_xy(k).wait_recv()
        rows[...] += trecv[k].astype(jnp.float32)
        return 0

    lax.fori_loop(1, NXY, sum_xy, 0)

    def scatter_z(k):
        there = (z + k) % NZ
        return remote(
            rows.at[pl.ds(pl.multiple_of(there * PIECE, PIECE), PIECE)],
            zrecv.at[k],
            rz_s.at[k],
            rz_r.at[k],
            at_z(k),
        )

    def start_scatter_z(k, _):
        scatter_z(k).start()
        return 0

    lax.fori_loop(1, NZ, start_scatter_z, 0)
    total = rows[pl.ds(pl.multiple_of(z * PIECE, PIECE), PIECE)]

    def sum_z(k, total):
        scatter_z(k).wait_recv()
        return total + zrecv[k]

    total = lax.fori_loop(1, NZ, sum_z, total) * scale
    here = pl.ds(pl.multiple_of(y * PIECE, PIECE), PIECE)
    sketch_ref[here] = total

    def gather_y(k):
        return remote(
            sketch_ref.at[here],
            sketch_ref.at[here],
            y_s.at[k],
            y_r.at[k],
            device(z, x, c, (y + k) % NY),
        )

    gsend[...] = jnp.dot(
        total.T, total, preferred_element_type=jnp.float32, precision=lax.Precision.HIGHEST
    ).reshape(gsend.shape)

    def scatter_g(k):
        px, py, pc = at_xyc(k)
        return remote(
            gsend.at[(px * NY + py) * NC + pc], grecv.at[k], g_s.at[k], g_r.at[k], dev_xyc(k)
        )

    def start_scatter_g(k, _):
        scatter_g(k).start()
        return 0

    lax.fori_loop(1, NXYC, start_scatter_g, 0)

    def start_gather_y(k, _):
        gather_y(k).start()
        return 0

    lax.fori_loop(1, NY, start_gather_y, 0)
    me = (x * NY + y) * NC + c

    def sum_g(k, acc):
        scatter_g(k).wait_recv()
        return acc + grecv[k]

    gz[z] = lax.fori_loop(1, NXYC, sum_g, gsend[me])

    def spread_z(k):
        return remote(gz.at[z], gz.at[z], gz_s.at[k], gz_r.at[k], at_z(k))

    def start_spread_z(k, _):
        spread_z(k).start()
        return 0

    def wait_spread_z(k, _):
        spread_z(k).wait()
        return 0

    lax.fori_loop(1, NZ, start_spread_z, 0)
    lax.fori_loop(1, NZ, wait_spread_z, 0)
    acc = gz[0]
    for k in range(1, NZ):
        acc = acc + gz[k]
    gram_ref[me] = acc

    def gather_g(k):
        return remote(gram_ref.at[me], gram_ref.at[me], ga_s.at[k], ga_r.at[k], dev_xyc(k))

    def start_gather_g(k, _):
        gather_g(k).start()
        return 0

    def wait_gather_g(k, _):
        gather_g(k).wait()
        return 0

    lax.fori_loop(1, NXYC, start_gather_g, 0)

    def end_xy(k, _):
        gather_xy(k).wait_send()
        scatter_xy(k).wait_send()
        return 0

    def end_z(k, _):
        scatter_z(k).wait_send()
        return 0

    def end_g(k, _):
        scatter_g(k).wait_send()
        return 0

    def end_y(k, _):
        gather_y(k).wait()
        return 0

    lax.fori_loop(1, NXY, end_xy, 0)
    lax.fori_loop(1, NZ, end_z, 0)
    lax.fori_loop(1, NXYC, end_g, 0)
    lax.fori_loop(1, NY, end_y, 0)
    lax.fori_loop(1, NXYC, wait_gather_g, 0)


def sketch_and_gram(frames, lengths, probes, devices):
    count, width = frames.shape
    columns = probes.shape[1]
    scale = 1.0 / math.sqrt(width * count * devices)
    half = width // NC
    dma = pltpu.SemaphoreType.DMA
    f32, bf16 = jnp.float32, jnp.bfloat16
    return pl.pallas_call(
        functools.partial(kernel, scale),
        out_shape=(
            jax.ShapeDtypeStruct((BLOCK, columns), f32),
            jax.ShapeDtypeStruct((NXYC, columns // NXYC, columns), f32),
        ),
        in_specs=[
            pl.BlockSpec(memory_space=pltpu.SMEM),
            pl.BlockSpec(memory_space=pl.ANY),
            pl.BlockSpec(memory_space=pl.ANY),
        ],
        out_specs=(pl.BlockSpec(memory_space=pltpu.VMEM), pl.BlockSpec(memory_space=pltpu.VMEM)),
        scratch_shapes=[
            pltpu.VMEM((NC * count, half), bf16),
            pltpu.VMEM((NX, NZ, NY, PIECE, NC * count), bf16),
            pltpu.VMEM((NX, NZ, NY, PIECE, columns), bf16),
            pltpu.VMEM((NC, count, BLOCK), f32),
            pltpu.VMEM((NC * count, columns), f32),
            pltpu.VMEM((NC * count, columns), f32),
            pltpu.VMEM((NC * count, columns), bf16),
            pltpu.VMEM((NXY, NZ * PIECE, columns), bf16),
            pltpu.VMEM((NXY, NZ * PIECE, columns), bf16),
            pltpu.VMEM((NZ * PIECE, columns), f32),
            pltpu.VMEM((NZ, PIECE, columns), f32),
            dma,
            dma,
            dma((2,)),
            dma((2,)),
            dma((2,)),
            dma((NZ,)),
            dma((NZ,)),
            dma((NXY,)),
            dma((NXY,)),
            dma((NXY,)),
            dma((NXY,)),
            dma((NZ,)),
            dma((NZ,)),
            dma((NY,)),
            dma((NY,)),
            pltpu.VMEM((NXYC, columns // NXYC, columns), f32),
            pltpu.VMEM((NXYC, columns // NXYC, columns), f32),
            pltpu.VMEM((NZ, columns // NXYC, columns), f32),
            dma((NXYC,)),
            dma((NXYC,)),
            dma((NZ,)),
            dma((NZ,)),
            dma((NXYC,)),
            dma((NXYC,)),
        ],
        compiler_params=pltpu.CompilerParams(
            collective_id=0, has_side_effects=True, vmem_limit_bytes=48 << 20
        ),
    )(lengths, frames, probes)


LANES = 128
PANEL = 8


def splat(v):
    return lax.broadcast_in_dim(v, (PANEL, LANES), (0, 1))


def less(x, y, z):
    return lax.sub(x, lax.mul(y, z))


def finish_kernel(scale, sketch, gram, basis, factor, a, b, inverse):
    n = gram.shape[0]
    panels = n // PANEL
    lane_tiles = n // LANES
    a[...] = gram[...]
    b[...] = jnp.where(
        lax.broadcasted_iota(jnp.int32, (n, n), 0) == lax.broadcasted_iota(jnp.int32, (n, n), 1),
        1.0,
        0.0,
    )

    def tile(ref, top, rows, t):
        return ref.at[top : top + rows, t * LANES : (t + 1) * LANES]

    one = jnp.ones((PANEL, LANES), jnp.float32)
    for p in range(panels):
        top = p * PANEL
        first = top // LANES
        tiles = [(a, t) for t in range(first, lane_tiles)] + [(b, t) for t in range(first + 1)]
        many = range(len(tiles))
        columns = [
            splat(a[top : top + PANEL, top + j : top + j + 1])
            for j in range(PANEL)
        ]
        d = [[splat(lax.slice(columns[j], (i, 0), (i + 1, LANES))) for j in range(i + 1)] for i in range(PANEL)]
        rows = [[splat(tile(ref, top + i, 1, t)[...]) for ref, t in tiles] for i in range(PANEL)]
        m = [[None] * PANEL for _ in range(PANEL)]
        inv = [None] * PANEL
        for j in range(PANEL):
            inv[j] = lax.div(one, d[j][j])
            for i in range(j + 1, PANEL):
                m[i][j] = lax.mul(d[i][j], inv[j])
            for i in range(j + 1, PANEL):
                for k in range(j + 1, i + 1):
                    d[i][k] = less(d[i][k], m[i][j], d[k][j])
                for k in many:
                    rows[i][k] = less(rows[i][k], m[i][j], rows[j][k])
        w = [None] * PANEL
        for i in reversed(range(PANEL)):
            w[i] = []
            for k in many:
                acc = lax.mul(inv[i], rows[i][k])
                for q in reversed(range(i + 1, PANEL)):
                    acc = less(acc, m[q][i], w[q][k])
                w[i].append(acc)

        def update(below, _):
            here = pl.ds(pl.multiple_of(below * PANEL, PANEL), PANEL)
            v = [splat(a[here, top + j : top + j + 1]) for j in range(PANEL)]
            for k, (ref, t) in enumerate(tiles):
                block = ref.at[here, t * LANES : (t + 1) * LANES]
                value = block[...]
                for j in range(PANEL):
                    value = less(value, v[j], w[j][k])
                block[...] = value
            return 0

        if p + 1 < panels:
            lax.fori_loop(p + 1, panels, update, 0, unroll=True)
        for i in range(PANEL):
            root = lax.rsqrt(d[i][i])
            for t in range(lane_tiles):
                upper = jnp.zeros((1, LANES), jnp.float32)
                lower = upper
                if t >= first:
                    upper = (rows[i][t - first] * root)[0:1]
                if t == first:
                    lane = lax.broadcasted_iota(jnp.int32, (1, LANES), 1) + t * LANES
                    upper = jnp.where(lane >= top + i, upper, 0.0)
                if t <= first:
                    lower = (rows[i][lane_tiles - first + t] * root)[0:1]
                tile(factor, top + i, 1, t)[...] = upper
                tile(inverse, top + i, 1, t)[...] = lower
    basis[...] = scale * lax.dot_general(
        sketch[...],
        inverse[...],
        (((1,), (1,)), ((), ())),
        precision=lax.Precision.HIGHEST,
        preferred_element_type=jnp.float32,
    )


def finish(sketch, gram, scale):
    return pl.pallas_call(
        functools.partial(finish_kernel, scale),
        out_shape=(
            jax.ShapeDtypeStruct(sketch.shape, jnp.float32),
            jax.ShapeDtypeStruct(gram.shape, jnp.float32),
        ),
        in_specs=[pl.BlockSpec(memory_space=pltpu.VMEM)] * 2,
        out_specs=(pl.BlockSpec(memory_space=pltpu.VMEM),) * 2,
        scratch_shapes=[pltpu.VMEM(gram.shape, jnp.float32)] * 3,
        compiler_params=pltpu.CompilerParams(vmem_limit_bytes=32 << 20),
    )(sketch, gram)


def shards(frames, lengths, probes):
    local = frames.reshape(frames.shape[2], frames.shape[3])
    width = local.shape[1]
    columns = probes.shape[1]
    devices = lax.axis_size("dp") * lax.axis_size("group")
    sketch, gram = sketch_and_gram(local, lengths, probes, devices)
    gram = gram.reshape(columns, columns)
    return finish(sketch, gram, math.sqrt(width))


def solution(mesh):
    placed = (P("dp", "group", None, None), P("dp", "group", None), P("dp", None))
    return jax.shard_map(
        shards, mesh=mesh, in_specs=placed, out_specs=(P("dp", None), P()), check_vma=False
    )
```

```python
import functools
import math

import jax
import jax.numpy as jnp
from jax import lax
from jax.experimental import pallas as pl
from jax.experimental.pallas import tpu as pltpu
from jax.sharding import PartitionSpec as P

MESH = pl.DeviceIdType.MESH
NZ, NX, NY, NC = 8, 4, 4, 2
NXY = NX * NY
NXYC = NXY * NC
BLOCK = 128
PIECE = BLOCK // NY
HALF = NZ // 2
ORDER = (1, 3, 2)


def device(z, x, c, y):
    return ((z * NX + x) * NC + c, y)


def remote(src, dst, send, recv, where):
    return pltpu.make_async_remote_copy(
        src_ref=src,
        dst_ref=dst,
        send_sem=send,
        recv_sem=recv,
        device_id=where,
        device_id_type=MESH,
    )


def kernel(
    scale,
    lengths,
    frames,
    probes,
    sketch_ref,
    gram_ref,
    lens,
    w,
    wt,
    pb,
    masks,
    part,
    other,
    paired,
    tsend,
    trecv,
    tsend2,
    trecv2,
    held,
    rows,
    zrecv,
    local_sem,
    probe_sem,
    lens_sem,
    frame_sems,
    mask_sems,
    part_sems,
    az_s,
    az_r,
    ap_s,
    ap_r,
    rs_s,
    rs_r,
    rs2_s,
    rs2_r,
    rz_s,
    rz_r,
    y_s,
    y_r,
    gsend,
    grecv,
    gz,
    g_s,
    g_r,
    gz_s,
    gz_r,
    ga_s,
    ga_r,
):
    dp = lax.axis_index("dp")
    y = lax.axis_index("group")
    c = dp % NC
    x = (dp // NC) % NX
    z = dp // (NC * NX)
    count = frames.shape[0]

    def at_z(k):
        return device((z + k) % NZ, x, c, y)

    def at_xyc(k):
        return (x + k // (NY * NC)) % NX, (y + (k // NC) % NY) % NY, (c + k % NC) % NC

    def dev_xyc(k):
        px, py, pc = at_xyc(k)
        return device(z, px, pc, py)

    partner = device(z, x, 1 - c, y)

    def own(i, _):
        col = ((i % NZ) * NX + i // NZ) * NC + c
        pltpu.make_async_copy(
            frames.at[:, pl.ds(pl.multiple_of(col * BLOCK, BLOCK), BLOCK)],
            w.at[pl.ds(pl.multiple_of(c * count, 128), count), pl.ds(pl.multiple_of(i * BLOCK, BLOCK), BLOCK)],
            local_sem,
        ).start()
        return 0

    mine = pltpu.make_async_copy(
        probes.at[pl.ds(pl.multiple_of(y * PIECE, PIECE), PIECE)], pb.at[x, z, y], probe_sem
    )
    mine.start()
    spans = pltpu.make_async_copy(lengths, lens, lens_sem)
    spans.start()
    lax.fori_loop(0, NZ * NX, own, 0)

    barrier = pltpu.get_barrier_semaphore()

    def greet_z(k, _):
        pl.semaphore_signal(barrier, inc=1, device_id=at_z(k), device_id_type=MESH)
        return 0

    def greet_xyc(k, _):
        pl.semaphore_signal(barrier, inc=1, device_id=dev_xyc(k), device_id_type=MESH)
        return 0

    lax.fori_loop(1, NZ, greet_z, 0)
    lax.fori_loop(1, NXYC, greet_xyc, 0)

    spans.wait()
    position = lax.broadcasted_iota(jnp.int32, (count, BLOCK), 0)
    inside = jnp.zeros((count, BLOCK), jnp.float32)
    start = jnp.int32(0)
    for span in range(4):
        end = start + lens[0, 0, span]
        inside = inside + jnp.where(
            jnp.logical_and(position >= start + 1, position <= end - 1), 1.0, 0.0
        )
        start = end
    masks[c] = inside

    pl.semaphore_wait(barrier, NZ - 1 + NXYC - 1)

    mine.wait()

    def gather_z(k):
        return remote(pb.at[x, z, y], pb.at[x, z, y], az_s.at[k], az_r.at[k], at_z(k))

    def start_gather_z(k, _):
        gather_z(k).start()
        return 0

    lax.fori_loop(1, NZ, start_gather_z, 0)

    def give(i, _):
        col = ((i % NZ) * NX + i // NZ) * NC + (1 - c)
        remote(
            frames.at[:, pl.ds(pl.multiple_of(col * BLOCK, BLOCK), BLOCK)],
            w.at[pl.ds(pl.multiple_of(c * count, 128), count), pl.ds(pl.multiple_of(i * BLOCK, BLOCK), BLOCK)],
            frame_sems.at[0],
            frame_sems.at[1],
            partner,
        ).start()
        return 0

    lax.fori_loop(0, NZ * NX, give, 0)
    mask_copy = remote(masks.at[c], masks.at[c], mask_sems.at[0], mask_sems.at[1], partner)
    mask_copy.start()

    def wait_gather_z(k, _):
        gather_z(k).wait()
        return 0

    lax.fori_loop(1, NZ, wait_gather_z, 0)

    def gather_xy(half, dx, dy):
        if half == 0:
            px, py = x, (y - dy + NY) % NY if dx else y
            where = device(z, (x + dx) % NX, c, y) if dx else device(z, x, c, (y + dy) % NY)
        else:
            px, py = (x - dx + NX) % NX if dy else x, y
            where = device(z, x, c, (y + dy) % NY) if dy else device(z, (x + dx) % NX, c, y)
        piece = pb.at[px, half * HALF : (half + 1) * HALF, py]
        return remote(piece, piece, ap_s.at[half, dx, dy], ap_r.at[half, dx, dy], where)

    for d in ORDER:
        gather_xy(0, 0, d).start()
        gather_xy(1, d, 0).start()
    for d in ORDER:
        gather_xy(0, d, 0).start()
        gather_xy(1, 0, d).start()

    def turn(i, _):
        block = w[:, pl.ds(pl.multiple_of(i * BLOCK, BLOCK), BLOCK)]
        wt[i // NZ, i % NZ] = block.T.reshape(NY, PIECE, 2 * count)
        return 0

    mine_rows = w.at[pl.ds(pl.multiple_of(c * count, 128), count)]
    pltpu.make_async_copy(mine_rows, mine_rows, local_sem).wait()
    frames_copy = remote(mine_rows, mine_rows, frame_sems.at[0], frame_sems.at[1], partner)

    for d in ORDER:
        gather_xy(0, 0, d).wait_recv()
        for e in ORDER:
            gather_xy(0, e, d).start()
        gather_xy(1, d, 0).wait_recv()
        for e in ORDER:
            gather_xy(1, d, e).start()
    frames_copy.wait()
    mask_copy.wait()
    lax.fori_loop(0, NZ * NX, turn, 0)

    depth = NZ * BLOCK
    for dx in (0,) + ORDER:
        for dy in ORDER:
            if dx:
                gather_xy(0, dx, dy).wait_recv()
            gather_xy(1, dx, dy).wait_recv()
        if dx:
            gather_xy(0, dx, 0).wait_recv()
        px = (x - dx + NX) % NX
        product = jnp.dot(
            w[:, pl.ds(pl.multiple_of(px * depth, depth), depth)],
            pb[px].reshape(depth, pb.shape[-1]),
            preferred_element_type=jnp.float32,
        )
        if dx == 0:
            part[...] = product
        else:
            part[...] += product

    swap = remote(part, other, part_sems.at[0], part_sems.at[1], partner)
    swap.start()
    swap.wait()
    shifted = pltpu.roll(part[...] + other[...], 1, 0)
    mask = masks[...].reshape(2 * count, BLOCK)
    mask = jnp.concatenate([mask, mask], axis=1)
    paired[...] = jnp.where(mask > 0.5, shifted, 0.0).astype(jnp.bfloat16)

    side = HALF * PIECE

    def scatter_1(half, dx, dy):
        where = device(z, x, c, (y + dy) % NY) if half else device(z, (x + dx) % NX, c, y)
        return remote(
            tsend.at[half, dx, dy],
            trecv.at[half, dx, dy],
            rs_s.at[half, dx, dy],
            rs_r.at[half, dx, dy],
            where,
        )

    def scatter_2(half, d):
        where = device(z, (x + d) % NX, c, y) if half else device(z, x, c, (y + d) % NY)
        return remote(
            tsend2.at[half, d], trecv2.at[half, d], rs2_s.at[half, d], rs2_r.at[half, d], where
        )

    both = [(dx, dy) for dx in ORDER for dy in ORDER]
    both += [(d, 0) for d in ORDER] + [(0, d) for d in ORDER] + [(0, 0)]
    for dx, dy in both:
        lhs = wt[(x + dx) % NX, :, (y + dy) % NY].reshape(NZ * PIECE, 2 * count)
        term = jnp.dot(lhs, paired[...], preferred_element_type=jnp.float32)
        for half, away, along in ((0, dx, dy), (1, dy, dx)):
            mine_term = term[half * side : (half + 1) * side]
            if away:
                tsend[half, dx, dy] = mine_term.astype(jnp.bfloat16)
                scatter_1(half, dx, dy).start()
            else:
                held[half, along] = mine_term

    def summed(half, along):
        total = held[half, along]
        for d in ORDER:
            at = (along, d) if half else (d, along)
            scatter_1(half, *at).wait_recv()
            total = total + trecv[half, at[0], at[1]].astype(jnp.float32)
        return total

    for d in ORDER:
        for half in range(2):
            tsend2[half, d] = summed(half, d).astype(jnp.bfloat16)
            scatter_2(half, d).start()
    for half in range(2):
        total = summed(half, 0)
        for d in ORDER:
            scatter_2(half, d).wait_recv()
            total = total + trecv2[half, d].astype(jnp.float32)
        rows[half * side : (half + 1) * side] = total

    def scatter_z(k):
        there = (z + k) % NZ
        return remote(
            rows.at[pl.ds(pl.multiple_of(there * PIECE, PIECE), PIECE)],
            zrecv.at[k],
            rz_s.at[k],
            rz_r.at[k],
            at_z(k),
        )

    def start_scatter_z(k, _):
        scatter_z(k).start()
        return 0

    lax.fori_loop(1, NZ, start_scatter_z, 0)
    total = rows[pl.ds(pl.multiple_of(z * PIECE, PIECE), PIECE)]

    def sum_z(k, total):
        scatter_z(k).wait_recv()
        return total + zrecv[k]

    total = lax.fori_loop(1, NZ, sum_z, total) * scale
    here = pl.ds(pl.multiple_of(y * PIECE, PIECE), PIECE)
    sketch_ref[here] = total

    def gather_y(k):
        return remote(
            sketch_ref.at[here],
            sketch_ref.at[here],
            y_s.at[k],
            y_r.at[k],
            device(z, x, c, (y + k) % NY),
        )

    gsend[...] = jnp.dot(
        total.T, total, preferred_element_type=jnp.float32, precision=lax.Precision.HIGHEST
    ).reshape(gsend.shape)

    def scatter_g(k):
        px, py, pc = at_xyc(k)
        return remote(
            gsend.at[(px * NY + py) * NC + pc], grecv.at[k], g_s.at[k], g_r.at[k], dev_xyc(k)
        )

    def start_scatter_g(k, _):
        scatter_g(k).start()
        return 0

    lax.fori_loop(1, NXYC, start_scatter_g, 0)

    def start_gather_y(k, _):
        gather_y(k).start()
        return 0

    lax.fori_loop(1, NY, start_gather_y, 0)
    me = (x * NY + y) * NC + c

    def sum_g(k, acc):
        scatter_g(k).wait_recv()
        return acc + grecv[k]

    gz[z] = lax.fori_loop(1, NXYC, sum_g, gsend[me])

    def spread_z(k):
        return remote(gz.at[z], gz.at[z], gz_s.at[k], gz_r.at[k], at_z(k))

    def start_spread_z(k, _):
        spread_z(k).start()
        return 0

    def wait_spread_z(k, _):
        spread_z(k).wait()
        return 0

    lax.fori_loop(1, NZ, start_spread_z, 0)
    lax.fori_loop(1, NZ, wait_spread_z, 0)
    acc = gz[0]
    for k in range(1, NZ):
        acc = acc + gz[k]
    gram_ref[me] = acc

    def gather_g(k):
        return remote(gram_ref.at[me], gram_ref.at[me], ga_s.at[k], ga_r.at[k], dev_xyc(k))

    def start_gather_g(k, _):
        gather_g(k).start()
        return 0

    def wait_gather_g(k, _):
        gather_g(k).wait()
        return 0

    lax.fori_loop(1, NXYC, start_gather_g, 0)

    def end_z(k, _):
        scatter_z(k).wait_send()
        return 0

    def end_g(k, _):
        scatter_g(k).wait_send()
        return 0

    def end_y(k, _):
        gather_y(k).wait()
        return 0

    for half in range(2):
        for dx in range(NX):
            for dy in range(NY):
                if dx or dy:
                    gather_xy(half, dx, dy).wait_send()
                if (dy if half else dx):
                    scatter_1(half, dx, dy).wait_send()
        for d in ORDER:
            scatter_2(half, d).wait_send()
    lax.fori_loop(1, NZ, end_z, 0)
    lax.fori_loop(1, NXYC, end_g, 0)
    lax.fori_loop(1, NY, end_y, 0)
    lax.fori_loop(1, NXYC, wait_gather_g, 0)


def sketch_and_gram(frames, lengths, probes, devices):
    count, width = frames.shape
    columns = probes.shape[1]
    scale = 1.0 / math.sqrt(width * count * devices)
    half = width // NC
    dma = pltpu.SemaphoreType.DMA
    f32, bf16 = jnp.float32, jnp.bfloat16
    return pl.pallas_call(
        functools.partial(kernel, scale),
        out_shape=(
            jax.ShapeDtypeStruct((BLOCK, columns), f32),
            jax.ShapeDtypeStruct((NXYC, columns // NXYC, columns), f32),
        ),
        in_specs=[
            pl.BlockSpec(memory_space=pltpu.HBM),
            pl.BlockSpec(memory_space=pltpu.HBM),
            pl.BlockSpec(memory_space=pltpu.HBM),
        ],
        out_specs=(pl.BlockSpec(memory_space=pltpu.VMEM), pl.BlockSpec(memory_space=pltpu.VMEM)),
        scratch_shapes=[
            pltpu.SMEM((1, 1, 4), jnp.int32),
            pltpu.VMEM((NC * count, half), bf16),
            pltpu.VMEM((NX, NZ, NY, PIECE, NC * count), bf16),
            pltpu.VMEM((NX, NZ, NY, PIECE, columns), bf16),
            pltpu.VMEM((NC, count, BLOCK), f32),
            pltpu.VMEM((NC * count, columns), f32),
            pltpu.VMEM((NC * count, columns), f32),
            pltpu.VMEM((NC * count, columns), bf16),
            pltpu.VMEM((2, NX, NY, HALF * PIECE, columns), bf16),
            pltpu.VMEM((2, NX, NY, HALF * PIECE, columns), bf16),
            pltpu.VMEM((2, NX, HALF * PIECE, columns), bf16),
            pltpu.VMEM((2, NX, HALF * PIECE, columns), bf16),
            pltpu.VMEM((2, NX, HALF * PIECE, columns), f32),
            pltpu.VMEM((NZ * PIECE, columns), f32),
            pltpu.VMEM((NZ, PIECE, columns), f32),
            dma,
            dma,
            dma,
            dma((2,)),
            dma((2,)),
            dma((2,)),
            dma((NZ,)),
            dma((NZ,)),
            dma((2, NX, NY)),
            dma((2, NX, NY)),
            dma((2, NX, NY)),
            dma((2, NX, NY)),
            dma((2, NX)),
            dma((2, NX)),
            dma((NZ,)),
            dma((NZ,)),
            dma((NY,)),
            dma((NY,)),
            pltpu.VMEM((NXYC, columns // NXYC, columns), f32),
            pltpu.VMEM((NXYC, columns // NXYC, columns), f32),
            pltpu.VMEM((NZ, columns // NXYC, columns), f32),
            dma((NXYC,)),
            dma((NXYC,)),
            dma((NZ,)),
            dma((NZ,)),
            dma((NXYC,)),
            dma((NXYC,)),
        ],
        compiler_params=pltpu.CompilerParams(
            collective_id=0, has_side_effects=True, vmem_limit_bytes=48 << 20
        ),
    )(lengths, frames, probes)


LANES = 128
PANEL = 8


def splat(v):
    return lax.broadcast_in_dim(v, (PANEL, LANES), (0, 1))


def less(x, y, z):
    return lax.sub(x, lax.mul(y, z))


def finish_kernel(scale, sketch, gram, basis, factor, a, b, inverse):
    n = gram.shape[0]
    panels = n // PANEL
    lane_tiles = n // LANES
    a[...] = gram[...]
    b[...] = jnp.where(
        lax.broadcasted_iota(jnp.int32, (n, n), 0) == lax.broadcasted_iota(jnp.int32, (n, n), 1),
        1.0,
        0.0,
    )

    def tile(ref, top, rows, t):
        return ref.at[top : top + rows, t * LANES : (t + 1) * LANES]

    one = jnp.ones((PANEL, LANES), jnp.float32)
    for p in range(panels):
        top = p * PANEL
        first = top // LANES
        tiles = [(a, t) for t in range(first, lane_tiles)] + [(b, t) for t in range(first + 1)]
        many = range(len(tiles))
        columns = [
            splat(a[top : top + PANEL, top + j : top + j + 1])
            for j in range(PANEL)
        ]
        d = [[splat(lax.slice(columns[j], (i, 0), (i + 1, LANES))) for j in range(i + 1)] for i in range(PANEL)]
        rows = [[splat(tile(ref, top + i, 1, t)[...]) for ref, t in tiles] for i in range(PANEL)]
        m = [[None] * PANEL for _ in range(PANEL)]
        inv = [None] * PANEL
        for j in range(PANEL):
            inv[j] = lax.div(one, d[j][j])
            for i in range(j + 1, PANEL):
                m[i][j] = lax.mul(d[i][j], inv[j])
            for i in range(j + 1, PANEL):
                for k in range(j + 1, i + 1):
                    d[i][k] = less(d[i][k], m[i][j], d[k][j])
                for k in many:
                    rows[i][k] = less(rows[i][k], m[i][j], rows[j][k])
        w = [None] * PANEL
        for i in reversed(range(PANEL)):
            w[i] = []
            for k in many:
                acc = lax.mul(inv[i], rows[i][k])
                for q in reversed(range(i + 1, PANEL)):
                    acc = less(acc, m[q][i], w[q][k])
                w[i].append(acc)

        def update(below, _):
            here = pl.ds(pl.multiple_of(below * PANEL, PANEL), PANEL)
            v = [splat(a[here, top + j : top + j + 1]) for j in range(PANEL)]
            for k, (ref, t) in enumerate(tiles):
                block = ref.at[here, t * LANES : (t + 1) * LANES]
                value = block[...]
                for j in range(PANEL):
                    value = less(value, v[j], w[j][k])
                block[...] = value
            return 0

        if p + 1 < panels:
            lax.fori_loop(p + 1, panels, update, 0, unroll=True)
        for i in range(PANEL):
            root = lax.rsqrt(d[i][i])
            for t in range(lane_tiles):
                upper = jnp.zeros((1, LANES), jnp.float32)
                lower = upper
                if t >= first:
                    upper = (rows[i][t - first] * root)[0:1]
                if t == first:
                    lane = lax.broadcasted_iota(jnp.int32, (1, LANES), 1) + t * LANES
                    upper = jnp.where(lane >= top + i, upper, 0.0)
                if t <= first:
                    lower = (rows[i][lane_tiles - first + t] * root)[0:1]
                tile(factor, top + i, 1, t)[...] = upper
                tile(inverse, top + i, 1, t)[...] = lower
    basis[...] = scale * lax.dot_general(
        sketch[...],
        inverse[...],
        (((1,), (1,)), ((), ())),
        precision=lax.Precision.HIGHEST,
        preferred_element_type=jnp.float32,
    )


def finish(sketch, gram, scale):
    return pl.pallas_call(
        functools.partial(finish_kernel, scale),
        out_shape=(
            jax.ShapeDtypeStruct(sketch.shape, jnp.float32),
            jax.ShapeDtypeStruct(gram.shape, jnp.float32),
        ),
        in_specs=[pl.BlockSpec(memory_space=pltpu.VMEM)] * 2,
        out_specs=(pl.BlockSpec(memory_space=pltpu.VMEM),) * 2,
        scratch_shapes=[pltpu.VMEM(gram.shape, jnp.float32)] * 3,
        compiler_params=pltpu.CompilerParams(vmem_limit_bytes=32 << 20),
    )(sketch, gram)


def shards(frames, lengths, probes):
    local = frames.reshape(frames.shape[2], frames.shape[3])
    width = local.shape[1]
    columns = probes.shape[1]
    devices = lax.axis_size("dp") * lax.axis_size("group")
    lengths = pltpu.with_memory_space_constraint(lengths, pltpu.HBM)
    probes = pltpu.with_memory_space_constraint(probes, pltpu.HBM)
    sketch, gram = sketch_and_gram(local, lengths, probes, devices)
    gram = gram.reshape(columns, columns)
    return finish(sketch, gram, math.sqrt(width))


def solution(mesh):
    placed = (P("dp", "group", None, None), P("dp", "group", None), P("dp", None))
    return jax.shard_map(
        shards, mesh=mesh, in_specs=placed, out_specs=(P("dp", None), P()), check_vma=False
    )
```

```python
import functools
import itertools
import math

import jax
import jax.numpy as jnp
from jax import lax
from jax.experimental import pallas as pl
from jax.experimental.pallas import tpu as pltpu
from jax.sharding import PartitionSpec as P

MESH = pl.DeviceIdType.MESH
NZ, NX, NY, NC = 8, 4, 4, 2
NXY = NX * NY
NXYC = NXY * NC
BLOCK = 128
PIECE = BLOCK // NY
HALF = NZ // 2
ORDER = (1, 3, 2)
Z_ORDER = (4, 3, 5, 2, 6, 1, 7)
XYC_ORDER = sorted(
    (k for k in itertools.product(range(NX), range(NY), range(NC)) if any(k)),
    key=lambda k: -min(k[0], NX - k[0]) - min(k[1], NY - k[1]),
)
TURNS = (14, 18, 26)


def device(z, x, c, y):
    return ((z * NX + x) * NC + c, y)


def remote(src, dst, send, recv, where):
    return pltpu.make_async_remote_copy(
        src_ref=src,
        dst_ref=dst,
        send_sem=send,
        recv_sem=recv,
        device_id=where,
        device_id_type=MESH,
    )


def kernel(
    scale,
    lengths,
    frames,
    probes,
    sketch_ref,
    gram_ref,
    lens,
    w,
    wt,
    pb,
    masks,
    part,
    other,
    paired,
    tsend,
    trecv,
    tsend2,
    trecv2,
    held,
    rows,
    zrecv,
    local_sem,
    probe_sem,
    lens_sem,
    frame_sems,
    mask_sems,
    part_sems,
    az_s,
    az_r,
    ap_s,
    ap_r,
    rs_s,
    rs_r,
    rs2_s,
    rs2_r,
    rz_s,
    rz_r,
    y_s,
    y_r,
    gsend,
    grecv,
    gz,
    g_s,
    g_r,
    gz_s,
    gz_r,
    ga_s,
    ga_r,
):
    dp = lax.axis_index("dp")
    y = lax.axis_index("group")
    c = dp % NC
    x = (dp // NC) % NX
    z = dp // (NC * NX)
    count = frames.shape[0]

    xs = [x] + [(x + d) % NX for d in range(1, NX)]
    ys = [y] + [(y + d) % NY for d in range(1, NY)]
    cs = [c, 1 - c]
    zs = [z] + [(z + d) % NZ for d in range(1, NZ)]

    def at_z(k):
        return device(zs[k], x, c, y)

    def place(k):
        dx, dy, dc = k
        return (xs[dx] * NY + ys[dy]) * NC + cs[dc]

    def at_xyc(k):
        dx, dy, dc = k
        return device(z, xs[dx], cs[dc], ys[dy])

    partner = device(z, x, 1 - c, y)

    barrier = pltpu.get_barrier_semaphore()
    for k in XYC_ORDER:
        pl.semaphore_signal(barrier, inc=1, device_id=at_xyc(k), device_id_type=MESH)
    for k in Z_ORDER:
        pl.semaphore_signal(barrier, inc=1, device_id=at_z(k), device_id_type=MESH)

    def own(i, _):
        col = ((i % NZ) * NX + i // NZ) * NC + c
        pltpu.make_async_copy(
            frames.at[:, pl.ds(pl.multiple_of(col * BLOCK, BLOCK), BLOCK)],
            w.at[pl.ds(pl.multiple_of(c * count, 128), count), pl.ds(pl.multiple_of(i * BLOCK, BLOCK), BLOCK)],
            local_sem,
        ).start()
        return 0

    mine = pltpu.make_async_copy(
        probes.at[pl.ds(pl.multiple_of(y * PIECE, PIECE), PIECE)], pb.at[x, z, y], probe_sem
    )
    mine.start()
    spans = pltpu.make_async_copy(lengths, lens, lens_sem)
    spans.start()
    lax.fori_loop(0, NZ * NX, own, 0)

    spans.wait()
    position = lax.broadcasted_iota(jnp.int32, (count, BLOCK), 0)
    inside = jnp.zeros((count, BLOCK), jnp.float32)
    start = jnp.int32(0)
    for span in range(4):
        end = start + lens[0, 0, span]
        inside = inside + jnp.where(
            jnp.logical_and(position >= start + 1, position <= end - 1), 1.0, 0.0
        )
        start = end
    masks[c] = inside

    pl.semaphore_wait(barrier, NZ - 1 + NXYC - 1)

    mine.wait()

    def gather_z(k):
        return remote(pb.at[x, z, y], pb.at[x, z, y], az_s.at[k], az_r.at[k], at_z(k))

    for k in Z_ORDER:
        gather_z(k).start()

    def give(i, _):
        col = ((i % NZ) * NX + i // NZ) * NC + (1 - c)
        remote(
            frames.at[:, pl.ds(pl.multiple_of(col * BLOCK, BLOCK), BLOCK)],
            w.at[pl.ds(pl.multiple_of(c * count, 128), count), pl.ds(pl.multiple_of(i * BLOCK, BLOCK), BLOCK)],
            frame_sems.at[0],
            frame_sems.at[1],
            partner,
        ).start()
        return 0

    lax.fori_loop(0, NZ * NX, give, 0)
    mask_copy = remote(masks.at[c], masks.at[c], mask_sems.at[0], mask_sems.at[1], partner)
    mask_copy.start()

    for k in Z_ORDER:
        gather_z(k).wait_recv()

    def gather_xy(half, dx, dy):
        if half == 0:
            px, py = x, (y - dy + NY) % NY if dx else y
            where = device(z, (x + dx) % NX, c, y) if dx else device(z, x, c, (y + dy) % NY)
        else:
            px, py = (x - dx + NX) % NX if dy else x, y
            where = device(z, x, c, (y + dy) % NY) if dy else device(z, (x + dx) % NX, c, y)
        piece = pb.at[px, half * HALF : (half + 1) * HALF, py]
        return remote(piece, piece, ap_s.at[half, dx, dy], ap_r.at[half, dx, dy], where)

    for d in ORDER:
        gather_xy(0, 0, d).start()
        gather_xy(1, d, 0).start()
    for d in ORDER:
        gather_xy(0, d, 0).start()
        gather_xy(1, 0, d).start()

    def turn(i, _):
        at = pl.ds(pl.multiple_of(i * BLOCK, BLOCK), BLOCK)
        block = w[:, at]
        wt[i // NZ, i % NZ] = block.T.reshape(NY, PIECE, 2 * count)
        moved = pltpu.roll(block.astype(jnp.float32), 1, 0)
        keep = masks[...].reshape(2 * count, BLOCK) > 0.5
        w[:, at] = jnp.where(keep, moved, 0.0).astype(jnp.bfloat16)
        return 0

    mine_rows = w.at[pl.ds(pl.multiple_of(c * count, 128), count)]
    pltpu.make_async_copy(mine_rows, mine_rows, local_sem).wait()
    frames_copy = remote(mine_rows, mine_rows, frame_sems.at[0], frame_sems.at[1], partner)
    frames_copy.wait()
    mask_copy.wait()

    turned = 0
    for d, until in zip(ORDER, TURNS):
        lax.fori_loop(turned, until, turn, 0)
        turned = until
        gather_xy(0, 0, d).wait_recv()
        for e in ORDER:
            gather_xy(0, e, d).start()
        gather_xy(1, d, 0).wait_recv()
        for e in ORDER:
            gather_xy(1, d, e).start()
    lax.fori_loop(turned, NZ * NX, turn, 0)

    def swap(core):
        return remote(
            part.at[core], other.at[core], part_sems.at[0, core], part_sems.at[1, core], partner
        )

    depth = NZ * BLOCK
    for dx in (0,) + ORDER:
        for dy in ORDER:
            if dx:
                gather_xy(0, dx, dy).wait_recv()
            gather_xy(1, dx, dy).wait_recv()
        if dx:
            gather_xy(0, dx, 0).wait_recv()
        px = (x - dx + NX) % NX
        block = pb[px].reshape(depth, pb.shape[-1])
        for core in range(NC):
            its = slice(core * count, (core + 1) * count)
            product = jnp.dot(
                w[its, pl.ds(pl.multiple_of(px * depth, depth), depth)],
                block,
                preferred_element_type=jnp.float32,
            )
            if dx == 0:
                part[core] = product
            else:
                part[core] += product
            if dx == ORDER[-1]:
                swap(core).start()
    for core in range(NC):
        swap(core).wait()
        paired[core * count : (core + 1) * count] = (part[core] + other[core]).astype(jnp.bfloat16)

    side = HALF * PIECE

    def scatter_1(half, dx, dy):
        where = device(z, x, c, (y + dy) % NY) if half else device(z, (x + dx) % NX, c, y)
        return remote(
            tsend.at[half, dx, dy],
            trecv.at[half, dx, dy],
            rs_s.at[half, dx, dy],
            rs_r.at[half, dx, dy],
            where,
        )

    def scatter_2(half, d):
        where = device(z, (x + d) % NX, c, y) if half else device(z, x, c, (y + d) % NY)
        return remote(
            tsend2.at[half, d], trecv2.at[half, d], rs2_s.at[half, d], rs2_r.at[half, d], where
        )

    both = [(dx, dy) for dx in ORDER for dy in ORDER]
    both += [(d, 0) for d in ORDER] + [(0, d) for d in ORDER] + [(0, 0)]
    for dx, dy in both:
        lhs = wt[(x + dx) % NX, :, (y + dy) % NY].reshape(NZ * PIECE, 2 * count)
        term = jnp.dot(lhs, paired[...], preferred_element_type=jnp.float32)
        for half, away, along in ((0, dx, dy), (1, dy, dx)):
            mine_term = term[half * side : (half + 1) * side]
            if away:
                tsend[half, dx, dy] = mine_term.astype(jnp.bfloat16)
                scatter_1(half, dx, dy).start()
            else:
                held[half, along] = mine_term

    def summed(half, along):
        total = held[half, along]
        for d in ORDER:
            at = (along, d) if half else (d, along)
            scatter_1(half, *at).wait_recv()
            total = total + trecv[half, at[0], at[1]].astype(jnp.float32)
        return total

    for d in ORDER:
        for half in range(2):
            tsend2[half, d] = summed(half, d).astype(jnp.bfloat16)
            scatter_2(half, d).start()
    for half in range(2):
        total = summed(half, 0)
        for d in ORDER:
            scatter_2(half, d).wait_recv()
            total = total + trecv2[half, d].astype(jnp.float32)
        rows[half * side : (half + 1) * side] = total

    def scatter_z(k):
        there = zs[k]
        return remote(
            rows.at[pl.ds(pl.multiple_of(there * PIECE, PIECE), PIECE)],
            zrecv.at[k],
            rz_s.at[k],
            rz_r.at[k],
            at_z(k),
        )

    for k in Z_ORDER:
        scatter_z(k).start()
    total = rows[pl.ds(pl.multiple_of(z * PIECE, PIECE), PIECE)]
    for k in reversed(Z_ORDER):
        scatter_z(k).wait_recv()
        total = total + zrecv[k]
    total = total * scale
    here = pl.ds(pl.multiple_of(y * PIECE, PIECE), PIECE)
    sketch_ref[here] = total

    def gather_y(k):
        return remote(
            sketch_ref.at[here],
            sketch_ref.at[here],
            y_s.at[k],
            y_r.at[k],
            device(z, x, c, ys[k]),
        )

    gsend[...] = jnp.dot(
        total.T, total, preferred_element_type=jnp.float32, precision=lax.Precision.HIGHEST
    ).reshape(gsend.shape)

    def scatter_g(k):
        i = XYC_ORDER.index(k)
        return remote(gsend.at[place(k)], grecv.at[i], g_s.at[i], g_r.at[i], at_xyc(k))

    for k in XYC_ORDER:
        scatter_g(k).start()
    me = place((0, 0, 0))
    acc = gsend[me]
    for k in reversed(XYC_ORDER):
        scatter_g(k).wait_recv()
        acc = acc + grecv[XYC_ORDER.index(k)]
    gz[z] = acc

    def spread_z(k):
        return remote(gz.at[z], gz.at[z], gz_s.at[k], gz_r.at[k], at_z(k))

    for k in Z_ORDER:
        spread_z(k).start()
    for k in ORDER:
        gather_y(k).start()
    for k in Z_ORDER:
        spread_z(k).wait_recv()
    acc = gz[0]
    for k in range(1, NZ):
        acc = acc + gz[k]
    gram_ref[me] = acc

    def gather_g(k):
        i = XYC_ORDER.index(k)
        return remote(gram_ref.at[me], gram_ref.at[me], ga_s.at[i], ga_r.at[i], at_xyc(k))

    for k in XYC_ORDER:
        gather_g(k).start()

    for half in range(2):
        for dx in range(NX):
            for dy in range(NY):
                if dx or dy:
                    gather_xy(half, dx, dy).wait_send()
                if (dy if half else dx):
                    scatter_1(half, dx, dy).wait_send()
        for d in ORDER:
            scatter_2(half, d).wait_send()
    for k in Z_ORDER:
        gather_z(k).wait_send()
        scatter_z(k).wait_send()
        spread_z(k).wait_send()
    for k in XYC_ORDER:
        scatter_g(k).wait_send()
    for k in ORDER:
        gather_y(k).wait()
    for k in reversed(XYC_ORDER):
        gather_g(k).wait()


def sketch_and_gram(frames, lengths, probes, devices):
    count, width = frames.shape
    columns = probes.shape[1]
    scale = 1.0 / math.sqrt(width * count * devices)
    half = width // NC
    dma = pltpu.SemaphoreType.DMA
    f32, bf16 = jnp.float32, jnp.bfloat16
    return pl.pallas_call(
        functools.partial(kernel, scale),
        out_shape=(
            jax.ShapeDtypeStruct((BLOCK, columns), f32),
            jax.ShapeDtypeStruct((NXYC, columns // NXYC, columns), f32),
        ),
        in_specs=[
            pl.BlockSpec(memory_space=pltpu.HBM),
            pl.BlockSpec(memory_space=pltpu.HBM),
            pl.BlockSpec(memory_space=pltpu.HBM),
        ],
        out_specs=(pl.BlockSpec(memory_space=pltpu.VMEM), pl.BlockSpec(memory_space=pltpu.VMEM)),
        scratch_shapes=[
            pltpu.SMEM((1, 1, 4), jnp.int32),
            pltpu.VMEM((NC * count, half), bf16),
            pltpu.VMEM((NX, NZ, NY, PIECE, NC * count), bf16),
            pltpu.VMEM((NX, NZ, NY, PIECE, columns), bf16),
            pltpu.VMEM((NC, count, BLOCK), f32),
            pltpu.VMEM((NC, count, columns), f32),
            pltpu.VMEM((NC, count, columns), f32),
            pltpu.VMEM((NC * count, columns), bf16),
            pltpu.VMEM((2, NX, NY, HALF * PIECE, columns), bf16),
            pltpu.VMEM((2, NX, NY, HALF * PIECE, columns), bf16),
            pltpu.VMEM((2, NX, HALF * PIECE, columns), bf16),
            pltpu.VMEM((2, NX, HALF * PIECE, columns), bf16),
            pltpu.VMEM((2, NX, HALF * PIECE, columns), f32),
            pltpu.VMEM((NZ * PIECE, columns), f32),
            pltpu.VMEM((NZ, PIECE, columns), f32),
            dma,
            dma,
            dma,
            dma((2,)),
            dma((2,)),
            dma((2, NC)),
            dma((NZ,)),
            dma((NZ,)),
            dma((2, NX, NY)),
            dma((2, NX, NY)),
            dma((2, NX, NY)),
            dma((2, NX, NY)),
            dma((2, NX)),
            dma((2, NX)),
            dma((NZ,)),
            dma((NZ,)),
            dma((NY,)),
            dma((NY,)),
            pltpu.VMEM((NXYC, columns // NXYC, columns), f32),
            pltpu.VMEM((NXYC, columns // NXYC, columns), f32),
            pltpu.VMEM((NZ, columns // NXYC, columns), f32),
            dma((NXYC,)),
            dma((NXYC,)),
            dma((NZ,)),
            dma((NZ,)),
            dma((NXYC,)),
            dma((NXYC,)),
        ],
        compiler_params=pltpu.CompilerParams(
            collective_id=0, has_side_effects=True, vmem_limit_bytes=48 << 20
        ),
    )(lengths, frames, probes)


LANES = 128
PANEL = 8


def splat(v):
    return lax.broadcast_in_dim(v, (PANEL, LANES), (0, 1))


def less(x, y, z):
    return lax.sub(x, lax.mul(y, z))


def finish_kernel(scale, sketch, gram, basis, factor, a, b, inverse):
    n = gram.shape[0]
    panels = n // PANEL
    lane_tiles = n // LANES
    a[...] = gram[...]
    b[...] = jnp.where(
        lax.broadcasted_iota(jnp.int32, (n, n), 0) == lax.broadcasted_iota(jnp.int32, (n, n), 1),
        1.0,
        0.0,
    )

    def tile(ref, top, rows, t):
        return ref.at[top : top + rows, t * LANES : (t + 1) * LANES]

    one = jnp.ones((PANEL, LANES), jnp.float32)
    for p in range(panels):
        top = p * PANEL
        first = top // LANES
        tiles = [(a, t) for t in range(first, lane_tiles)] + [(b, t) for t in range(first + 1)]
        many = range(len(tiles))
        d = [[splat(a[top + i : top + i + 1, top + j : top + j + 1]) for j in range(i + 1)] for i in range(PANEL)]
        rows = [[splat(tile(ref, top + i, 1, t)[...]) for ref, t in tiles] for i in range(PANEL)]
        m = [[None] * PANEL for _ in range(PANEL)]
        inv = [None] * PANEL
        for j in range(PANEL):
            inv[j] = lax.div(one, d[j][j])
            for i in range(j + 1, PANEL):
                m[i][j] = lax.mul(d[i][j], inv[j])
            for i in range(j + 1, PANEL):
                for k in range(j + 1, i + 1):
                    d[i][k] = less(d[i][k], m[i][j], d[k][j])
                for k in many:
                    rows[i][k] = less(rows[i][k], m[i][j], rows[j][k])
        w = [None] * PANEL
        for i in reversed(range(PANEL)):
            w[i] = []
            for k in many:
                acc = lax.mul(inv[i], rows[i][k])
                for q in reversed(range(i + 1, PANEL)):
                    acc = less(acc, m[q][i], w[q][k])
                w[i].append(acc)

        def update(below, _):
            here = pl.ds(pl.multiple_of(below * PANEL, PANEL), PANEL)
            v = [splat(a[here, top + j : top + j + 1]) for j in range(PANEL)]
            for k, (ref, t) in enumerate(tiles):
                block = ref.at[here, t * LANES : (t + 1) * LANES]
                value = block[...]
                for j in range(PANEL):
                    value = less(value, v[j], w[j][k])
                block[...] = value
            return 0

        last = (first + 1) * LANES // PANEL
        if p + 1 < last:
            lax.fori_loop(p + 1, last, update, 0, unroll=True)
        for i in range(PANEL):
            root = lax.rsqrt(d[i][i])
            for t in range(lane_tiles):
                upper = jnp.zeros((1, LANES), jnp.float32)
                lower = upper
                if t >= first:
                    upper = (rows[i][t - first] * root)[0:1]
                if t == first:
                    lane = lax.broadcasted_iota(jnp.int32, (1, LANES), 1) + t * LANES
                    upper = jnp.where(lane >= top + i, upper, 0.0)
                if t <= first:
                    lower = (rows[i][lane_tiles - first + t] * root)[0:1]
                tile(factor, top + i, 1, t)[...] = upper
                tile(inverse, top + i, 1, t)[...] = lower
        if p + 1 == last and last < panels:
            done, below = top + PANEL - LANES, top + PANEL
            right = factor[done:below, below:]
            taken = lax.dot_general(
                right,
                jnp.concatenate([inverse[done:below, :below], right], axis=1),
                (((0,), (0,)), ((), ())),
                precision=lax.Precision.HIGHEST,
                preferred_element_type=jnp.float32,
            )
            b[below:, :below] = b[below:, :below] - taken[:, :below]
            a[below:, below:] = a[below:, below:] - taken[:, below:]
    basis[...] = scale * lax.dot_general(
        sketch[...],
        inverse[...],
        (((1,), (1,)), ((), ())),
        precision=lax.Precision.HIGHEST,
        preferred_element_type=jnp.float32,
    )


def finish(sketch, gram, scale):
    return pl.pallas_call(
        functools.partial(finish_kernel, scale),
        out_shape=(
            jax.ShapeDtypeStruct(sketch.shape, jnp.float32),
            jax.ShapeDtypeStruct(gram.shape, jnp.float32),
        ),
        in_specs=[pl.BlockSpec(memory_space=pltpu.VMEM)] * 2,
        out_specs=(pl.BlockSpec(memory_space=pltpu.VMEM),) * 2,
        scratch_shapes=[pltpu.VMEM(gram.shape, jnp.float32)] * 3,
        compiler_params=pltpu.CompilerParams(vmem_limit_bytes=32 << 20),
    )(sketch, gram)


def shards(frames, lengths, probes):
    local = frames.reshape(frames.shape[2], frames.shape[3])
    width = local.shape[1]
    columns = probes.shape[1]
    devices = lax.axis_size("dp") * lax.axis_size("group")
    lengths = pltpu.with_memory_space_constraint(lengths, pltpu.HBM)
    probes = pltpu.with_memory_space_constraint(probes, pltpu.HBM)
    sketch, gram = sketch_and_gram(local, lengths, probes, devices)
    gram = gram.reshape(columns, columns)
    return finish(sketch, gram, math.sqrt(width))


def solution(mesh):
    placed = (P("dp", "group", None, None), P("dp", "group", None), P("dp", None))
    return jax.shard_map(
        shards, mesh=mesh, in_specs=placed, out_specs=(P("dp", None), P()), check_vma=False
    )
```

```python
import functools
import itertools
import math

import jax
import jax.numpy as jnp
from jax import lax
from jax.experimental import pallas as pl
from jax.experimental.pallas import tpu as pltpu
from jax.sharding import PartitionSpec as P

MESH = pl.DeviceIdType.MESH
NZ, NX, NY, NC = 8, 4, 4, 2
NXY = NX * NY
NXYC = NXY * NC
BLOCK = 128
PIECE = BLOCK // NY
PAIR = 2
GROUPS = NZ // PAIR
ORDER = (1, 3, 2)
REL = (0, 1, 7, 2, 6, 3, 5, 4)
SLOT = tuple(REL.index(k) for k in range(NZ))
Z_ORDER = (4, 3, 5, 2, 6, 1, 7)
XYC_ORDER = sorted(
    (k for k in itertools.product(range(NX), range(NY), range(NC)) if any(k)),
    key=lambda k: -min(k[0], NX - k[0]) - min(k[1], NY - k[1]),
)
TURNS = (18, 22, 27)


def device(z, x, c, y):
    return ((z * NX + x) * NC + c, y)


def remote(src, dst, send, recv, where):
    return pltpu.make_async_remote_copy(
        src_ref=src,
        dst_ref=dst,
        send_sem=send,
        recv_sem=recv,
        device_id=where,
        device_id_type=MESH,
    )


def kernel(
    scale,
    lengths,
    frames,
    probes,
    sketch_ref,
    gram_ref,
    lens,
    w,
    wt,
    pb,
    masks,
    part,
    other,
    paired,
    tsend,
    trecv,
    tsend2,
    trecv2,
    held,
    rows,
    zrecv,
    local_sem,
    probe_sem,
    lens_sem,
    frame_sems,
    mask_sems,
    part_sems,
    az_s,
    az_r,
    ap_s,
    ap_r,
    rs_s,
    rs_r,
    rs2_s,
    rs2_r,
    rz_s,
    rz_r,
    y_s,
    y_r,
    gsend,
    grecv,
    gz,
    g_s,
    g_r,
    gz_s,
    gz_r,
    ga_s,
    ga_r,
):
    dp = lax.axis_index("dp")
    y = lax.axis_index("group")
    c = dp % NC
    x = (dp // NC) % NX
    z = dp // (NC * NX)
    count = frames.shape[0]

    xs = [x] + [(x + d) % NX for d in range(1, NX)]
    ys = [y] + [(y + d) % NY for d in range(1, NY)]
    cs = [c, 1 - c]
    zs = [z] + [(z + d) % NZ for d in range(1, NZ)]

    def at_z(k):
        return device(zs[k], x, c, y)

    def place(k):
        dx, dy, dc = k
        return (xs[dx] * NY + ys[dy]) * NC + cs[dc]

    def at_xyc(k):
        dx, dy, dc = k
        return device(z, xs[dx], cs[dc], ys[dy])

    partner = device(z, x, 1 - c, y)

    barrier = pltpu.get_barrier_semaphore()
    for k in XYC_ORDER:
        pl.semaphore_signal(barrier, inc=1, device_id=at_xyc(k), device_id_type=MESH)
    for k in Z_ORDER:
        pl.semaphore_signal(barrier, inc=1, device_id=at_z(k), device_id_type=MESH)

    def columns_of(s, i, core):
        return pl.ds(pl.multiple_of(((zs[-REL[s]] * NX + i) * NC + core) * BLOCK, BLOCK), BLOCK)

    def places_of(s, i):
        at = pl.ds(pl.multiple_of((i * NZ + s) * BLOCK, BLOCK), BLOCK)
        return w.at[pl.ds(pl.multiple_of(c * count, 128), count), at]

    mine = pltpu.make_async_copy(
        probes.at[pl.ds(pl.multiple_of(y * PIECE, PIECE), PIECE)], pb.at[x, 0, y], probe_sem
    )
    mine.start()
    spans = pltpu.make_async_copy(lengths, lens, lens_sem)
    spans.start()
    for s in range(NZ):

        def own(i, _, s=s):
            pltpu.make_async_copy(
                frames.at[:, columns_of(s, i, c)], places_of(s, i), local_sem
            ).start()
            return 0

        lax.fori_loop(0, NX, own, 0)

    spans.wait()
    position = lax.broadcasted_iota(jnp.int32, (count, BLOCK), 0)
    inside = jnp.zeros((count, BLOCK), jnp.float32)
    start = jnp.int32(0)
    for span in range(4):
        end = start + lens[0, 0, span]
        inside = inside + jnp.where(
            jnp.logical_and(position >= start + 1, position <= end - 1), 1.0, 0.0
        )
        start = end
    masks[c] = inside

    pl.semaphore_wait(barrier, NZ - 1 + NXYC - 1)

    mine.wait()

    def gather_z(k):
        return remote(pb.at[x, 0, y], pb.at[x, SLOT[k], y], az_s.at[k], az_r.at[k], at_z(k))

    for k in REL[1:]:
        gather_z(k).start()

    for s in range(NZ):

        def give(i, _, s=s):
            remote(
                frames.at[:, columns_of(s, i, 1 - c)],
                places_of(s, i),
                frame_sems.at[0],
                frame_sems.at[1],
                partner,
            ).start()
            return 0

        lax.fori_loop(0, NX, give, 0)
    mask_copy = remote(masks.at[c], masks.at[c], mask_sems.at[0], mask_sems.at[1], partner)
    mask_copy.start()

    def gather_xy(group, dx, dy):
        if group % 2 == 0:
            px, py = x, ys[-dy] if dx else y
            where = device(z, xs[dx], c, y) if dx else device(z, x, c, ys[dy])
        else:
            px, py = xs[-dx] if dy else x, y
            where = device(z, x, c, ys[dy]) if dy else device(z, xs[dx], c, y)
        piece = pb.at[px, group * PAIR : (group + 1) * PAIR, py]
        return remote(piece, piece, ap_s.at[group, dx, dy], ap_r.at[group, dx, dy], where)

    def leg(group, first, second):
        return gather_xy(group, *((second, first) if group % 2 == 0 else (first, second)))

    for group in range(GROUPS):
        for slot in range(max(1, group * PAIR), (group + 1) * PAIR):
            gather_z(REL[slot]).wait_recv()
        for d in ORDER:
            leg(group, d, 0).start()
        for d in ORDER:
            leg(group, 0, d).start()

    def turn(i, _):
        at = pl.ds(pl.multiple_of(i * BLOCK, BLOCK), BLOCK)
        block = w[:, at]
        wt[i // NZ, i % NZ] = block.T.reshape(NY, PIECE, 2 * count)
        moved = pltpu.roll(block.astype(jnp.float32), 1, 0)
        keep = masks[...].reshape(2 * count, BLOCK) > 0.5
        w[:, at] = jnp.where(keep, moved, 0.0).astype(jnp.bfloat16)
        return 0

    def forward(group, d):
        leg(group, d, 0).wait_recv()
        for e in ORDER:
            leg(group, d, e).start()

    for d in ORDER:
        forward(0, d)
        forward(1, d)
    mine_rows = w.at[pl.ds(pl.multiple_of(c * count, 128), count)]
    pltpu.make_async_copy(mine_rows, mine_rows, local_sem).wait()
    frames_copy = remote(mine_rows, mine_rows, frame_sems.at[0], frame_sems.at[1], partner)
    frames_copy.wait()
    mask_copy.wait()
    turned = 0
    for d, until in zip(ORDER, TURNS):
        lax.fori_loop(turned, until, turn, 0)
        turned = until
        forward(2, d)
        forward(3, d)
    lax.fori_loop(turned, NZ * NX, turn, 0)

    def swap(core):
        return remote(
            part.at[core], other.at[core], part_sems.at[0, core], part_sems.at[1, core], partner
        )

    depth = NZ * BLOCK
    for dx in (0,) + ORDER:
        for group in range(GROUPS):
            for dy in range(NY):
                if (dx if group % 2 == 0 else dy):
                    gather_xy(group, dx, dy).wait_recv()
        px = xs[-dx]
        block = pb[px].reshape(depth, pb.shape[-1])
        for core in range(NC):
            its = slice(core * count, (core + 1) * count)
            product = jnp.dot(
                w[its, pl.ds(pl.multiple_of(px * depth, depth), depth)],
                block,
                preferred_element_type=jnp.float32,
            )
            if dx == 0:
                part[core] = product
            else:
                part[core] += product
            if dx == ORDER[-1]:
                swap(core).start()
    for core in range(NC):
        swap(core).wait()
        paired[core * count : (core + 1) * count] = (part[core] + other[core]).astype(jnp.bfloat16)

    side = PAIR * PIECE

    def scatter_1(group, dx, dy):
        where = device(z, x, c, ys[dy]) if group % 2 else device(z, xs[dx], c, y)
        return remote(
            tsend.at[group, dx, dy],
            trecv.at[group, dx, dy],
            rs_s.at[group, dx, dy],
            rs_r.at[group, dx, dy],
            where,
        )

    def scatter_2(group, d):
        where = device(z, xs[d], c, y) if group % 2 else device(z, x, c, ys[d])
        return remote(
            tsend2.at[group, d], trecv2.at[group, d], rs2_s.at[group, d], rs2_r.at[group, d], where
        )

    def scatter_z(s):
        return remote(
            rows.at[s * PIECE : (s + 1) * PIECE],
            zrecv.at[s],
            rz_s.at[s],
            rz_r.at[s],
            at_z(NZ - REL[s]),
        )

    both = [(dx, dy) for dx in ORDER for dy in ORDER]
    both += [(d, 0) for d in ORDER] + [(0, d) for d in ORDER] + [(0, 0)]
    for groups in ((2, 3), (0, 1)):
        for dx, dy in both:
            slots = slice(groups[0] * PAIR, (groups[1] + 1) * PAIR)
            lhs = wt[xs[dx], slots, ys[dy]].reshape(2 * side, 2 * count)
            term = jnp.dot(lhs, paired[...], preferred_element_type=jnp.float32)
            for group, away, along in ((groups[0], dx, dy), (groups[1], dy, dx)):
                mine_term = term[(group % 2) * side : (group % 2 + 1) * side]
                if away:
                    tsend[group, dx, dy] = mine_term.astype(jnp.bfloat16)
                    scatter_1(group, dx, dy).start()
                else:
                    held[group, along] = mine_term

    def summed(group, along):
        total = held[group, along]
        for d in ORDER:
            at = (along, d) if group % 2 else (d, along)
            scatter_1(group, *at).wait_recv()
            total = total + trecv[group, at[0], at[1]].astype(jnp.float32)
        return total

    for groups in ((2, 3), (0, 1)):
        for d in ORDER:
            for group in groups:
                tsend2[group, d] = summed(group, d).astype(jnp.bfloat16)
                scatter_2(group, d).start()
        for group in groups:
            total = summed(group, 0)
            for d in ORDER:
                scatter_2(group, d).wait_recv()
                total = total + trecv2[group, d].astype(jnp.float32)
            rows[group * side : (group + 1) * side] = total
            for slot in reversed(range(max(1, group * PAIR), (group + 1) * PAIR)):
                scatter_z(slot).start()

    total = rows[:PIECE]
    for slot in reversed(range(1, NZ)):
        scatter_z(slot).wait_recv()
        total = total + zrecv[slot]
    total = total * scale
    here = pl.ds(pl.multiple_of(y * PIECE, PIECE), PIECE)
    sketch_ref[here] = total

    def gather_y(k):
        return remote(
            sketch_ref.at[here],
            sketch_ref.at[here],
            y_s.at[k],
            y_r.at[k],
            device(z, x, c, ys[k]),
        )

    gsend[...] = jnp.dot(
        total.T, total, preferred_element_type=jnp.float32, precision=lax.Precision.HIGHEST
    ).reshape(gsend.shape)

    def scatter_g(k):
        i = XYC_ORDER.index(k)
        return remote(gsend.at[place(k)], grecv.at[i], g_s.at[i], g_r.at[i], at_xyc(k))

    for k in XYC_ORDER:
        scatter_g(k).start()
    me = place((0, 0, 0))
    acc = gsend[me]
    for k in reversed(XYC_ORDER):
        scatter_g(k).wait_recv()
        acc = acc + grecv[XYC_ORDER.index(k)]
    gz[z] = acc

    def spread_z(k):
        return remote(gz.at[z], gz.at[z], gz_s.at[k], gz_r.at[k], at_z(k))

    for k in Z_ORDER:
        spread_z(k).start()
    for k in ORDER:
        gather_y(k).start()
    for k in Z_ORDER:
        spread_z(k).wait_recv()
    acc = gz[0]
    for k in range(1, NZ):
        acc = acc + gz[k]
    gram_ref[me] = acc

    def gather_g(k):
        i = XYC_ORDER.index(k)
        return remote(gram_ref.at[me], gram_ref.at[me], ga_s.at[i], ga_r.at[i], at_xyc(k))

    for k in XYC_ORDER:
        gather_g(k).start()

    for group in range(GROUPS):
        for dx in range(NX):
            for dy in range(NY):
                if dx or dy:
                    gather_xy(group, dx, dy).wait_send()
                if (dy if group % 2 else dx):
                    scatter_1(group, dx, dy).wait_send()
        for d in ORDER:
            scatter_2(group, d).wait_send()
    for k in Z_ORDER:
        gather_z(k).wait_send()
        scatter_z(k).wait_send()
        spread_z(k).wait_send()
    for k in XYC_ORDER:
        scatter_g(k).wait_send()
    for k in ORDER:
        gather_y(k).wait()
    for k in reversed(XYC_ORDER):
        gather_g(k).wait()


def sketch_and_gram(frames, lengths, probes, devices):
    count, width = frames.shape
    columns = probes.shape[1]
    scale = 1.0 / math.sqrt(width * count * devices)
    half = width // NC
    dma = pltpu.SemaphoreType.DMA
    f32, bf16 = jnp.float32, jnp.bfloat16
    return pl.pallas_call(
        functools.partial(kernel, scale),
        out_shape=(
            jax.ShapeDtypeStruct((BLOCK, columns), f32),
            jax.ShapeDtypeStruct((NXYC, columns // NXYC, columns), f32),
        ),
        in_specs=[
            pl.BlockSpec(memory_space=pltpu.HBM),
            pl.BlockSpec(memory_space=pltpu.HBM),
            pl.BlockSpec(memory_space=pltpu.HBM),
        ],
        out_specs=(pl.BlockSpec(memory_space=pltpu.VMEM), pl.BlockSpec(memory_space=pltpu.VMEM)),
        scratch_shapes=[
            pltpu.SMEM((1, 1, 4), jnp.int32),
            pltpu.VMEM((NC * count, half), bf16),
            pltpu.VMEM((NX, NZ, NY, PIECE, NC * count), bf16),
            pltpu.VMEM((NX, NZ, NY, PIECE, columns), bf16),
            pltpu.VMEM((NC, count, BLOCK), f32),
            pltpu.VMEM((NC, count, columns), f32),
            pltpu.VMEM((NC, count, columns), f32),
            pltpu.VMEM((NC * count, columns), bf16),
            pltpu.VMEM((GROUPS, NX, NY, PAIR * PIECE, columns), bf16),
            pltpu.VMEM((GROUPS, NX, NY, PAIR * PIECE, columns), bf16),
            pltpu.VMEM((GROUPS, NX, PAIR * PIECE, columns), bf16),
            pltpu.VMEM((GROUPS, NX, PAIR * PIECE, columns), bf16),
            pltpu.VMEM((GROUPS, NX, PAIR * PIECE, columns), f32),
            pltpu.VMEM((NZ * PIECE, columns), f32),
            pltpu.VMEM((NZ, PIECE, columns), f32),
            dma,
            dma,
            dma,
            dma((2,)),
            dma((2,)),
            dma((2, NC)),
            dma((NZ,)),
            dma((NZ,)),
            dma((GROUPS, NX, NY)),
            dma((GROUPS, NX, NY)),
            dma((GROUPS, NX, NY)),
            dma((GROUPS, NX, NY)),
            dma((GROUPS, NX)),
            dma((GROUPS, NX)),
            dma((NZ,)),
            dma((NZ,)),
            dma((NY,)),
            dma((NY,)),
            pltpu.VMEM((NXYC, columns // NXYC, columns), f32),
            pltpu.VMEM((NXYC, columns // NXYC, columns), f32),
            pltpu.VMEM((NZ, columns // NXYC, columns), f32),
            dma((NXYC,)),
            dma((NXYC,)),
            dma((NZ,)),
            dma((NZ,)),
            dma((NXYC,)),
            dma((NXYC,)),
        ],
        compiler_params=pltpu.CompilerParams(
            collective_id=0, has_side_effects=True, vmem_limit_bytes=48 << 20
        ),
    )(lengths, frames, probes)


LANES = 128
PANEL = 8


def splat(v):
    return lax.broadcast_in_dim(v, (PANEL, LANES), (0, 1))


def less(x, y, z):
    return lax.sub(x, lax.mul(y, z))


def finish_kernel(scale, sketch, gram, basis, factor, a, b, inverse):
    n = gram.shape[0]
    panels = n // PANEL
    lane_tiles = n // LANES
    a[...] = gram[...]
    b[...] = jnp.where(
        lax.broadcasted_iota(jnp.int32, (n, n), 0) == lax.broadcasted_iota(jnp.int32, (n, n), 1),
        1.0,
        0.0,
    )

    def tile(ref, top, rows, t):
        return ref.at[top : top + rows, t * LANES : (t + 1) * LANES]

    one = jnp.ones((PANEL, LANES), jnp.float32)
    for p in range(panels):
        top = p * PANEL
        first = top // LANES
        tiles = [(a, t) for t in range(first, lane_tiles)] + [(b, t) for t in range(first + 1)]
        many = range(len(tiles))
        d = [[splat(a[top + i : top + i + 1, top + j : top + j + 1]) for j in range(i + 1)] for i in range(PANEL)]
        rows = [[splat(tile(ref, top + i, 1, t)[...]) for ref, t in tiles] for i in range(PANEL)]
        m = [[None] * PANEL for _ in range(PANEL)]
        inv = [None] * PANEL
        for j in range(PANEL):
            inv[j] = lax.div(one, d[j][j])
            for i in range(j + 1, PANEL):
                m[i][j] = lax.mul(d[i][j], inv[j])
            for i in range(j + 1, PANEL):
                for k in range(j + 1, i + 1):
                    d[i][k] = less(d[i][k], m[i][j], d[k][j])
                for k in many:
                    rows[i][k] = less(rows[i][k], m[i][j], rows[j][k])
        w = [None] * PANEL
        for i in reversed(range(PANEL)):
            w[i] = []
            for k in many:
                acc = lax.mul(inv[i], rows[i][k])
                for q in reversed(range(i + 1, PANEL)):
                    acc = less(acc, m[q][i], w[q][k])
                w[i].append(acc)

        def update(below, _):
            here = pl.ds(pl.multiple_of(below * PANEL, PANEL), PANEL)
            v = [splat(a[here, top + j : top + j + 1]) for j in range(PANEL)]
            for k, (ref, t) in enumerate(tiles):
                block = ref.at[here, t * LANES : (t + 1) * LANES]
                value = block[...]
                for j in range(PANEL):
                    value = less(value, v[j], w[j][k])
                block[...] = value
            return 0

        last = (first + 1) * LANES // PANEL
        if p + 1 < last:
            lax.fori_loop(p + 1, last, update, 0, unroll=True)
        for i in range(PANEL):
            root = lax.rsqrt(d[i][i])
            for t in range(lane_tiles):
                upper = jnp.zeros((1, LANES), jnp.float32)
                lower = upper
                if t >= first:
                    upper = (rows[i][t - first] * root)[0:1]
                if t == first:
                    lane = lax.broadcasted_iota(jnp.int32, (1, LANES), 1) + t * LANES
                    upper = jnp.where(lane >= top + i, upper, 0.0)
                if t <= first:
                    lower = (rows[i][lane_tiles - first + t] * root)[0:1]
                tile(factor, top + i, 1, t)[...] = upper
                tile(inverse, top + i, 1, t)[...] = lower
        if p + 1 == last and last < panels:
            done, below = top + PANEL - LANES, top + PANEL
            right = factor[done:below, below:]
            taken = lax.dot_general(
                right,
                jnp.concatenate([inverse[done:below, :below], right], axis=1),
                (((0,), (0,)), ((), ())),
                precision=lax.Precision.HIGHEST,
                preferred_element_type=jnp.float32,
            )
            b[below:, :below] = b[below:, :below] - taken[:, :below]
            a[below:, below:] = a[below:, below:] - taken[:, below:]
    basis[...] = scale * lax.dot_general(
        sketch[...],
        inverse[...],
        (((1,), (1,)), ((), ())),
        precision=lax.Precision.HIGHEST,
        preferred_element_type=jnp.float32,
    )


def finish(sketch, gram, scale):
    return pl.pallas_call(
        functools.partial(finish_kernel, scale),
        out_shape=(
            jax.ShapeDtypeStruct(sketch.shape, jnp.float32),
            jax.ShapeDtypeStruct(gram.shape, jnp.float32),
        ),
        in_specs=[pl.BlockSpec(memory_space=pltpu.VMEM)] * 2,
        out_specs=(pl.BlockSpec(memory_space=pltpu.VMEM),) * 2,
        scratch_shapes=[pltpu.VMEM(gram.shape, jnp.float32)] * 3,
        compiler_params=pltpu.CompilerParams(vmem_limit_bytes=32 << 20),
    )(sketch, gram)


def shards(frames, lengths, probes):
    local = frames.reshape(frames.shape[2], frames.shape[3])
    width = local.shape[1]
    columns = probes.shape[1]
    devices = lax.axis_size("dp") * lax.axis_size("group")
    lengths = pltpu.with_memory_space_constraint(lengths, pltpu.HBM)
    probes = pltpu.with_memory_space_constraint(probes, pltpu.HBM)
    sketch, gram = sketch_and_gram(local, lengths, probes, devices)
    gram = gram.reshape(columns, columns)
    return finish(sketch, gram, math.sqrt(width))


def solution(mesh):
    placed = (P("dp", "group", None, None), P("dp", "group", None), P("dp", None))
    return jax.shard_map(
        shards, mesh=mesh, in_specs=placed, out_specs=(P("dp", None), P()), check_vma=False
    )
```

```python
import functools
import itertools
import math

import jax
import jax.numpy as jnp
from jax import lax
from jax.experimental import pallas as pl
from jax.experimental.pallas import tpu as pltpu
from jax.sharding import PartitionSpec as P

MESH = pl.DeviceIdType.MESH
NZ, NX, NY, NC = 8, 4, 4, 2
NXY = NX * NY
NXYC = NXY * NC
BLOCK = 128
PIECE = BLOCK // NY
PAIR = 2
GROUPS = NZ // PAIR
ORDER = (1, 3, 2)
REL = (0, 1, 7, 2, 6, 3, 5, 4)
SLOT = tuple(REL.index(k) for k in range(NZ))
Z_ORDER = (4, 3, 5, 2, 6, 1, 7)
XYC_ORDER = sorted(
    (k for k in itertools.product(range(NX), range(NY), range(NC)) if any(k)),
    key=lambda k: -min(k[0], NX - k[0]) - min(k[1], NY - k[1]),
)
TURNS = (18, 22, 27)


def device(z, x, c, y):
    return ((z * NX + x) * NC + c, y)


def remote(src, dst, send, recv, where):
    return pltpu.make_async_remote_copy(
        src_ref=src,
        dst_ref=dst,
        send_sem=send,
        recv_sem=recv,
        device_id=where,
        device_id_type=MESH,
    )


def kernel(
    scale,
    lengths,
    frames,
    probes,
    sketch_ref,
    gram_ref,
    lens,
    w,
    wt,
    pb,
    masks,
    part,
    other,
    paired,
    tsend,
    trecv,
    tsend2,
    trecv2,
    held,
    rows,
    zrecv,
    local_sem,
    probe_sem,
    lens_sem,
    frame_sems,
    mask_sems,
    part_sems,
    az_s,
    az_r,
    ap_s,
    ap_r,
    rs_s,
    rs_r,
    rs2_s,
    rs2_r,
    rz_s,
    rz_r,
    y_s,
    y_r,
    gsend,
    grecv,
    gz,
    g_s,
    g_r,
    gz_s,
    gz_r,
    ga_s,
    ga_r,
):
    dp = lax.axis_index("dp")
    y = lax.axis_index("group")
    c = dp % NC
    x = (dp // NC) % NX
    z = dp // (NC * NX)
    count = frames.shape[0]

    xs = [x] + [(x + d) % NX for d in range(1, NX)]
    ys = [y] + [(y + d) % NY for d in range(1, NY)]
    cs = [c, 1 - c]
    zs = [z] + [(z + d) % NZ for d in range(1, NZ)]

    def at_z(k):
        return device(zs[k], x, c, y)

    def place(k):
        dx, dy, dc = k
        return (xs[dx] * NY + ys[dy]) * NC + cs[dc]

    def at_xyc(k):
        dx, dy, dc = k
        return device(z, xs[dx], cs[dc], ys[dy])

    partner = device(z, x, 1 - c, y)

    barrier = pltpu.get_barrier_semaphore()
    for k in XYC_ORDER:
        pl.semaphore_signal(barrier, inc=1, device_id=at_xyc(k), device_id_type=MESH)
    for k in Z_ORDER:
        pl.semaphore_signal(barrier, inc=1, device_id=at_z(k), device_id_type=MESH)

    def columns_of(s, i, core):
        return pl.ds(pl.multiple_of(((zs[-REL[s]] * NX + i) * NC + core) * BLOCK, BLOCK), BLOCK)

    def places_of(s, i):
        at = pl.ds(pl.multiple_of((i * NZ + s) * BLOCK, BLOCK), BLOCK)
        return w.at[pl.ds(pl.multiple_of(c * count, 128), count), at]

    mine = pltpu.make_async_copy(
        probes.at[pl.ds(pl.multiple_of(y * PIECE, PIECE), PIECE)], pb.at[x, 0, y], probe_sem
    )
    mine.start()
    spans = pltpu.make_async_copy(lengths, lens, lens_sem)
    spans.start()
    for s in range(NZ):

        def own(i, _, s=s):
            pltpu.make_async_copy(
                frames.at[:, columns_of(s, i, c)], places_of(s, i), local_sem
            ).start()
            return 0

        lax.fori_loop(0, NX, own, 0)

    spans.wait()
    position = lax.broadcasted_iota(jnp.int32, (count, BLOCK), 0)
    inside = jnp.zeros((count, BLOCK), jnp.float32)
    start = jnp.int32(0)
    for span in range(4):
        end = start + lens[0, 0, span]
        inside = inside + jnp.where(
            jnp.logical_and(position >= start + 1, position <= end - 1), 1.0, 0.0
        )
        start = end
    masks[c] = inside

    pl.semaphore_wait(barrier, NZ - 1 + NXYC - 1)

    mine.wait()

    def gather_z(k):
        return remote(pb.at[x, 0, y], pb.at[x, SLOT[k], y], az_s.at[k], az_r.at[k], at_z(k))

    for k in REL[1:]:
        gather_z(k).start()

    for s in range(NZ):

        def give(i, _, s=s):
            remote(
                frames.at[:, columns_of(s, i, 1 - c)],
                places_of(s, i),
                frame_sems.at[0],
                frame_sems.at[1],
                partner,
            ).start()
            return 0

        lax.fori_loop(0, NX, give, 0)
    mask_copy = remote(masks.at[c], masks.at[c], mask_sems.at[0], mask_sems.at[1], partner)
    mask_copy.start()

    def gather_xy(group, dx, dy):
        if group % 2 == 0:
            px, py = x, ys[-dy] if dx else y
            where = device(z, xs[dx], c, y) if dx else device(z, x, c, ys[dy])
        else:
            px, py = xs[-dx] if dy else x, y
            where = device(z, x, c, ys[dy]) if dy else device(z, xs[dx], c, y)
        piece = pb.at[px, group * PAIR : (group + 1) * PAIR, py]
        return remote(piece, piece, ap_s.at[group, dx, dy], ap_r.at[group, dx, dy], where)

    def leg(group, first, second):
        return gather_xy(group, *((second, first) if group % 2 == 0 else (first, second)))

    for group in range(GROUPS):
        for slot in range(max(1, group * PAIR), (group + 1) * PAIR):
            gather_z(REL[slot]).wait_recv()
        for d in ORDER:
            leg(group, d, 0).start()
        for d in ORDER:
            leg(group, 0, d).start()

    def turn(i, _):
        at = pl.ds(pl.multiple_of(i * BLOCK, BLOCK), BLOCK)
        block = w[:, at]
        wt[i // NZ, i % NZ] = block.T.reshape(NY, PIECE, 2 * count)
        moved = pltpu.roll(block.astype(jnp.float32), 1, 0)
        keep = masks[...].reshape(2 * count, BLOCK) > 0.5
        w[:, at] = jnp.where(keep, moved, 0.0).astype(jnp.bfloat16)
        return 0

    def forward(group, d):
        leg(group, d, 0).wait_recv()
        for e in ORDER:
            leg(group, d, e).start()

    for d in ORDER:
        forward(0, d)
        forward(1, d)
    mine_rows = w.at[pl.ds(pl.multiple_of(c * count, 128), count)]
    pltpu.make_async_copy(mine_rows, mine_rows, local_sem).wait()
    frames_copy = remote(mine_rows, mine_rows, frame_sems.at[0], frame_sems.at[1], partner)
    frames_copy.wait()
    mask_copy.wait()
    turned = 0
    for d, until in zip(ORDER, TURNS):
        lax.fori_loop(turned, until, turn, 0)
        turned = until
        forward(2, d)
        forward(3, d)
    lax.fori_loop(turned, NZ * NX, turn, 0)

    def swap(core):
        return remote(
            part.at[core], other.at[core], part_sems.at[0, core], part_sems.at[1, core], partner
        )

    depth = NZ * BLOCK
    for dx in (0,) + ORDER:
        for group in range(GROUPS):
            for dy in range(NY):
                if (dx if group % 2 == 0 else dy):
                    gather_xy(group, dx, dy).wait_recv()
        px = xs[-dx]
        block = pb[px].reshape(depth, pb.shape[-1])
        for core in range(NC):
            its = slice(core * count, (core + 1) * count)
            product = jnp.dot(
                w[its, pl.ds(pl.multiple_of(px * depth, depth), depth)],
                block,
                preferred_element_type=jnp.float32,
            )
            if dx == 0:
                part[core] = product
            else:
                part[core] += product
            if dx == ORDER[-1]:
                swap(core).start()
    for core in range(NC):
        swap(core).wait()
        paired[core * count : (core + 1) * count] = (part[core] + other[core]).astype(jnp.bfloat16)

    side = PAIR * PIECE

    def scatter_1(group, dx, dy):
        where = device(z, x, c, ys[dy]) if group % 2 else device(z, xs[dx], c, y)
        return remote(
            tsend.at[group, dx, dy],
            trecv.at[group, dx, dy],
            rs_s.at[group, dx, dy],
            rs_r.at[group, dx, dy],
            where,
        )

    def scatter_2(group, d):
        where = device(z, xs[d], c, y) if group % 2 else device(z, x, c, ys[d])
        return remote(
            tsend2.at[group, d], trecv2.at[group, d], rs2_s.at[group, d], rs2_r.at[group, d], where
        )

    def scatter_z(s):
        return remote(
            rows.at[s * PIECE : (s + 1) * PIECE],
            zrecv.at[s],
            rz_s.at[s],
            rz_r.at[s],
            at_z(NZ - REL[s]),
        )

    both = [(dx, dy) for dx in ORDER for dy in ORDER]
    both += [(d, 0) for d in ORDER] + [(0, d) for d in ORDER] + [(0, 0)]
    for groups in ((2, 3), (0, 1)):
        for dx, dy in both:
            slots = slice(groups[0] * PAIR, (groups[1] + 1) * PAIR)
            lhs = wt[xs[dx], slots, ys[dy]].reshape(2 * side, 2 * count)
            term = jnp.dot(lhs, paired[...], preferred_element_type=jnp.float32)
            for group, away, along in ((groups[0], dx, dy), (groups[1], dy, dx)):
                mine_term = term[(group % 2) * side : (group % 2 + 1) * side]
                if away:
                    tsend[group, dx, dy] = mine_term.astype(jnp.bfloat16)
                    scatter_1(group, dx, dy).start()
                else:
                    held[group, along] = mine_term

    def summed(group, along):
        total = held[group, along]
        for d in ORDER:
            at = (along, d) if group % 2 else (d, along)
            scatter_1(group, *at).wait_recv()
            total = total + trecv[group, at[0], at[1]].astype(jnp.float32)
        return total

    for groups in ((2, 3), (0, 1)):
        for d in ORDER:
            for group in groups:
                tsend2[group, d] = summed(group, d).astype(jnp.bfloat16)
                scatter_2(group, d).start()
        for group in groups:
            total = summed(group, 0)
            for d in ORDER:
                scatter_2(group, d).wait_recv()
                total = total + trecv2[group, d].astype(jnp.float32)
            rows[group * side : (group + 1) * side] = total
            for slot in reversed(range(max(1, group * PAIR), (group + 1) * PAIR)):
                scatter_z(slot).start()

    total = rows[:PIECE]
    for slot in reversed(range(1, NZ)):
        scatter_z(slot).wait_recv()
        total = total + zrecv[slot]
    total = total * scale
    here = pl.ds(pl.multiple_of(y * PIECE, PIECE), PIECE)
    sketch_ref[here] = total

    def gather_y(k):
        return remote(
            sketch_ref.at[here],
            sketch_ref.at[here],
            y_s.at[k],
            y_r.at[k],
            device(z, x, c, ys[k]),
        )

    gsend[...] = jnp.dot(
        total.T, total, preferred_element_type=jnp.float32, precision=lax.Precision.HIGHEST
    ).reshape(gsend.shape)

    def scatter_g(k):
        i = XYC_ORDER.index(k)
        return remote(gsend.at[place(k)], grecv.at[i], g_s.at[i], g_r.at[i], at_xyc(k))

    for k in XYC_ORDER:
        scatter_g(k).start()
    me = place((0, 0, 0))
    acc = gsend[me]
    for k in reversed(XYC_ORDER):
        scatter_g(k).wait_recv()
        acc = acc + grecv[XYC_ORDER.index(k)]
    gz[z] = acc

    def spread_z(k):
        return remote(gz.at[z], gz.at[z], gz_s.at[k], gz_r.at[k], at_z(k))

    for k in Z_ORDER:
        spread_z(k).start()
    for k in ORDER:
        gather_y(k).start()
    for k in Z_ORDER:
        spread_z(k).wait_recv()
    acc = gz[0]
    for k in range(1, NZ):
        acc = acc + gz[k]
    gram_ref[me] = acc

    def gather_g(k):
        i = XYC_ORDER.index(k)
        return remote(gram_ref.at[me], gram_ref.at[me], ga_s.at[i], ga_r.at[i], at_xyc(k))

    for k in XYC_ORDER:
        gather_g(k).start()

    for group in range(GROUPS):
        for dx in range(NX):
            for dy in range(NY):
                if dx or dy:
                    gather_xy(group, dx, dy).wait_send()
                if (dy if group % 2 else dx):
                    scatter_1(group, dx, dy).wait_send()
        for d in ORDER:
            scatter_2(group, d).wait_send()
    for k in Z_ORDER:
        gather_z(k).wait_send()
        scatter_z(k).wait_send()
        spread_z(k).wait_send()
    for k in XYC_ORDER:
        scatter_g(k).wait_send()
    for k in ORDER:
        gather_y(k).wait()
    for k in reversed(XYC_ORDER):
        gather_g(k).wait()


def sketch_and_gram(frames, lengths, probes, devices):
    count, width = frames.shape
    columns = probes.shape[1]
    scale = 1.0 / math.sqrt(width * count * devices)
    half = width // NC
    dma = pltpu.SemaphoreType.DMA
    f32, bf16 = jnp.float32, jnp.bfloat16
    return pl.pallas_call(
        functools.partial(kernel, scale),
        out_shape=(
            jax.ShapeDtypeStruct((BLOCK, columns), f32),
            jax.ShapeDtypeStruct((NXYC, columns // NXYC, columns), f32),
        ),
        in_specs=[
            pl.BlockSpec(memory_space=pltpu.HBM),
            pl.BlockSpec(memory_space=pltpu.HBM),
            pl.BlockSpec(memory_space=pltpu.HBM),
        ],
        out_specs=(pl.BlockSpec(memory_space=pltpu.VMEM), pl.BlockSpec(memory_space=pltpu.VMEM)),
        scratch_shapes=[
            pltpu.SMEM((1, 1, 4), jnp.int32),
            pltpu.VMEM((NC * count, half), bf16),
            pltpu.VMEM((NX, NZ, NY, PIECE, NC * count), bf16),
            pltpu.VMEM((NX, NZ, NY, PIECE, columns), bf16),
            pltpu.VMEM((NC, count, BLOCK), f32),
            pltpu.VMEM((NC, count, columns), f32),
            pltpu.VMEM((NC, count, columns), f32),
            pltpu.VMEM((NC * count, columns), bf16),
            pltpu.VMEM((GROUPS, NX, NY, PAIR * PIECE, columns), bf16),
            pltpu.VMEM((GROUPS, NX, NY, PAIR * PIECE, columns), bf16),
            pltpu.VMEM((GROUPS, NX, PAIR * PIECE, columns), bf16),
            pltpu.VMEM((GROUPS, NX, PAIR * PIECE, columns), bf16),
            pltpu.VMEM((GROUPS, NX, PAIR * PIECE, columns), f32),
            pltpu.VMEM((NZ * PIECE, columns), f32),
            pltpu.VMEM((NZ, PIECE, columns), f32),
            dma,
            dma,
            dma,
            dma((2,)),
            dma((2,)),
            dma((2, NC)),
            dma((NZ,)),
            dma((NZ,)),
            dma((GROUPS, NX, NY)),
            dma((GROUPS, NX, NY)),
            dma((GROUPS, NX, NY)),
            dma((GROUPS, NX, NY)),
            dma((GROUPS, NX)),
            dma((GROUPS, NX)),
            dma((NZ,)),
            dma((NZ,)),
            dma((NY,)),
            dma((NY,)),
            pltpu.VMEM((NXYC, columns // NXYC, columns), f32),
            pltpu.VMEM((NXYC, columns // NXYC, columns), f32),
            pltpu.VMEM((NZ, columns // NXYC, columns), f32),
            dma((NXYC,)),
            dma((NXYC,)),
            dma((NZ,)),
            dma((NZ,)),
            dma((NXYC,)),
            dma((NXYC,)),
        ],
        compiler_params=pltpu.CompilerParams(
            collective_id=0, has_side_effects=True, vmem_limit_bytes=48 << 20
        ),
    )(lengths, frames, probes)


LANES = 128
PANEL = 8


def splat(v):
    return lax.broadcast_in_dim(v, (PANEL, LANES), (0, 1))


def less(x, y, z):
    return lax.sub(x, lax.mul(y, z))


def finish_kernel(scale, sketch, gram, basis_out, factor_out, a, b, inverse, factor, basis, sems):
    n = gram.shape[0]
    panels = n // PANEL
    lane_tiles = n // LANES
    a[...] = gram[...]
    b[...] = jnp.where(
        lax.broadcasted_iota(jnp.int32, (n, n), 0) == lax.broadcasted_iota(jnp.int32, (n, n), 1),
        1.0,
        0.0,
    )

    def send(here, there, k):
        return pltpu.make_async_copy(here, there, sems.at[k])

    def tile(ref, top, rows, t):
        return ref.at[top : top + rows, t * LANES : (t + 1) * LANES]

    one = jnp.ones((PANEL, LANES), jnp.float32)
    for p in range(panels):
        top = p * PANEL
        first = top // LANES
        tiles = [(a, t) for t in range(first, lane_tiles)] + [(b, t) for t in range(first + 1)]
        many = range(len(tiles))
        d = [[splat(a[top + i : top + i + 1, top + j : top + j + 1]) for j in range(i + 1)] for i in range(PANEL)]
        rows = [[splat(tile(ref, top + i, 1, t)[...]) for ref, t in tiles] for i in range(PANEL)]
        m = [[None] * PANEL for _ in range(PANEL)]
        inv = [None] * PANEL
        for j in range(PANEL):
            inv[j] = lax.div(one, d[j][j])
            for i in range(j + 1, PANEL):
                m[i][j] = lax.mul(d[i][j], inv[j])
            for i in range(j + 1, PANEL):
                for k in range(j + 1, i + 1):
                    d[i][k] = less(d[i][k], m[i][j], d[k][j])
                for k in many:
                    rows[i][k] = less(rows[i][k], m[i][j], rows[j][k])
        w = [None] * PANEL
        for i in reversed(range(PANEL)):
            w[i] = []
            for k in many:
                acc = lax.mul(inv[i], rows[i][k])
                for q in reversed(range(i + 1, PANEL)):
                    acc = less(acc, m[q][i], w[q][k])
                w[i].append(acc)

        def update(below, _):
            here = pl.ds(pl.multiple_of(below * PANEL, PANEL), PANEL)
            v = [splat(a[here, top + j : top + j + 1]) for j in range(PANEL)]
            for k, (ref, t) in enumerate(tiles):
                block = ref.at[here, t * LANES : (t + 1) * LANES]
                value = block[...]
                for j in range(PANEL):
                    value = less(value, v[j], w[j][k])
                block[...] = value
            return 0

        last = (first + 1) * LANES // PANEL
        if p + 1 < last:
            lax.fori_loop(p + 1, last, update, 0, unroll=True)
        for i in range(PANEL):
            root = lax.rsqrt(d[i][i])
            for t in range(lane_tiles):
                upper = jnp.zeros((1, LANES), jnp.float32)
                lower = upper
                if t >= first:
                    upper = (rows[i][t - first] * root)[0:1]
                if t == first:
                    lane = lax.broadcasted_iota(jnp.int32, (1, LANES), 1) + t * LANES
                    upper = jnp.where(lane >= top + i, upper, 0.0)
                if t <= first:
                    lower = (rows[i][lane_tiles - first + t] * root)[0:1]
                tile(factor, top + i, 1, t)[...] = upper
                tile(inverse, top + i, 1, t)[...] = lower
        if p + 1 == last and last < panels:
            done, below = top + PANEL - LANES, top + PANEL
            right = factor[done:below, below:]
            taken = lax.dot_general(
                right,
                jnp.concatenate([inverse[done:below, :below], right], axis=1),
                (((0,), (0,)), ((), ())),
                precision=lax.Precision.HIGHEST,
                preferred_element_type=jnp.float32,
            )
            b[below:, :below] = b[below:, :below] - taken[:, :below]
            a[below:, below:] = a[below:, below:] - taken[:, below:]
        if p + 1 == last:
            send(factor.at[last * PANEL - LANES : last * PANEL], factor_out.at[last * PANEL - LANES : last * PANEL], 2 * first).start()
            basis[first] = scale * lax.dot_general(
                sketch[:, : last * PANEL],
                inverse[last * PANEL - LANES : last * PANEL, : last * PANEL],
                (((1,), (1,)), ((), ())),
                precision=lax.Precision.HIGHEST,
                preferred_element_type=jnp.float32,
            )
            send(basis.at[first], basis_out.at[:, last * PANEL - LANES : last * PANEL], 2 * first + 1).start()
    for t in range(lane_tiles):
        at = slice(t * LANES, (t + 1) * LANES)
        send(factor.at[at], factor_out.at[at], 2 * t).wait()
        send(basis.at[t], basis_out.at[:, at], 2 * t + 1).wait()


def finish(sketch, gram, scale):
    return pl.pallas_call(
        functools.partial(finish_kernel, scale),
        out_shape=(
            jax.ShapeDtypeStruct(sketch.shape, jnp.float32),
            jax.ShapeDtypeStruct(gram.shape, jnp.float32),
        ),
        in_specs=[pl.BlockSpec(memory_space=pltpu.VMEM)] * 2,
        out_specs=(pl.BlockSpec(memory_space=pltpu.HBM),) * 2,
        scratch_shapes=[pltpu.VMEM(gram.shape, jnp.float32)] * 4
        + [
            pltpu.VMEM((gram.shape[0] // LANES, sketch.shape[0], LANES), jnp.float32),
            pltpu.SemaphoreType.DMA((2 * gram.shape[0] // LANES,)),
        ],
        compiler_params=pltpu.CompilerParams(vmem_limit_bytes=32 << 20),
    )(sketch, gram)


def shards(frames, lengths, probes):
    local = frames.reshape(frames.shape[2], frames.shape[3])
    width = local.shape[1]
    columns = probes.shape[1]
    devices = lax.axis_size("dp") * lax.axis_size("group")
    lengths = pltpu.with_memory_space_constraint(lengths, pltpu.HBM)
    probes = pltpu.with_memory_space_constraint(probes, pltpu.HBM)
    sketch, gram = sketch_and_gram(local, lengths, probes, devices)
    gram = gram.reshape(columns, columns)
    return finish(sketch, gram, math.sqrt(width))


def solution(mesh):
    placed = (P("dp", "group", None, None), P("dp", "group", None), P("dp", None))
    return jax.shard_map(
        shards, mesh=mesh, in_specs=placed, out_specs=(P("dp", None), P()), check_vma=False
    )
```

```python
import functools
import itertools
import math

import jax
import jax.numpy as jnp
from jax import lax
from jax.experimental import pallas as pl
from jax.experimental.pallas import tpu as pltpu
from jax.sharding import PartitionSpec as P

MESH = pl.DeviceIdType.MESH
NZ, NX, NY, NC = 8, 4, 4, 2
NXY = NX * NY
NXYC = NXY * NC
BLOCK = 128
PIECE = BLOCK // NY
PAIR = 2
GROUPS = NZ // PAIR
ORDER = (1, 3, 2)
REL = (0, 1, 7, 2, 6, 3, 5, 4)
SLOT = tuple(REL.index(k) for k in range(NZ))
Z_ORDER = (4, 3, 5, 2, 6, 1, 7)
XYC_ORDER = sorted(
    (k for k in itertools.product(range(NX), range(NY), range(NC)) if any(k)),
    key=lambda k: -min(k[0], NX - k[0]) - min(k[1], NY - k[1]),
)
TURNS = (18, 22, 27)


def device(z, x, c, y):
    return ((z * NX + x) * NC + c, y)


def remote(src, dst, send, recv, where):
    return pltpu.make_async_remote_copy(
        src_ref=src,
        dst_ref=dst,
        send_sem=send,
        recv_sem=recv,
        device_id=where,
        device_id_type=MESH,
    )


def kernel(
    scale,
    lengths,
    frames,
    probes,
    sketch_ref,
    gram_ref,
    lens,
    w,
    wt,
    pb,
    masks,
    part,
    other,
    paired,
    tsend,
    trecv,
    tsend2,
    trecv2,
    held,
    rows,
    zrecv,
    local_sem,
    probe_sem,
    lens_sem,
    frame_sems,
    mask_sems,
    part_sems,
    az_s,
    az_r,
    ap_s,
    ap_r,
    rs_s,
    rs_r,
    rs2_s,
    rs2_r,
    rz_s,
    rz_r,
    y_s,
    y_r,
    gsend,
    grecv,
    gz,
    g_s,
    g_r,
    gz_s,
    gz_r,
    ga_s,
    ga_r,
):
    dp = lax.axis_index("dp")
    y = lax.axis_index("group")
    c = dp % NC
    x = (dp // NC) % NX
    z = dp // (NC * NX)
    count = frames.shape[0]

    xs = [x] + [(x + d) % NX for d in range(1, NX)]
    ys = [y] + [(y + d) % NY for d in range(1, NY)]
    cs = [c, 1 - c]
    zs = [z] + [(z + d) % NZ for d in range(1, NZ)]

    def at_z(k):
        return device(zs[k], x, c, y)

    def place(k):
        dx, dy, dc = k
        return (xs[dx] * NY + ys[dy]) * NC + cs[dc]

    def at_xyc(k):
        dx, dy, dc = k
        return device(z, xs[dx], cs[dc], ys[dy])

    partner = device(z, x, 1 - c, y)

    barrier = pltpu.get_barrier_semaphore()
    for k in XYC_ORDER:
        pl.semaphore_signal(barrier, inc=1, device_id=at_xyc(k), device_id_type=MESH)
    for k in Z_ORDER:
        pl.semaphore_signal(barrier, inc=1, device_id=at_z(k), device_id_type=MESH)

    def columns_of(s, i, core):
        return pl.ds(pl.multiple_of(((zs[-REL[s]] * NX + i) * NC + core) * BLOCK, BLOCK), BLOCK)

    def places_of(s, i):
        at = pl.ds(pl.multiple_of((i * NZ + s) * BLOCK, BLOCK), BLOCK)
        return w.at[pl.ds(pl.multiple_of(c * count, 128), count), at]

    mine = pltpu.make_async_copy(
        probes.at[pl.ds(pl.multiple_of(y * PIECE, PIECE), PIECE)], pb.at[x, 0, y], probe_sem
    )
    mine.start()
    spans = pltpu.make_async_copy(lengths, lens, lens_sem)
    spans.start()
    for s in range(NZ):

        def own(i, _, s=s):
            pltpu.make_async_copy(
                frames.at[:, columns_of(s, i, c)], places_of(s, i), local_sem
            ).start()
            return 0

        lax.fori_loop(0, NX, own, 0)

    spans.wait()
    position = lax.broadcasted_iota(jnp.int32, (count, BLOCK), 0)
    inside = jnp.zeros((count, BLOCK), jnp.float32)
    start = jnp.int32(0)
    for span in range(4):
        end = start + lens[0, 0, span]
        inside = inside + jnp.where(
            jnp.logical_and(position >= start + 1, position <= end - 1), 1.0, 0.0
        )
        start = end
    masks[c] = inside

    pl.semaphore_wait(barrier, NZ - 1 + NXYC - 1)

    mine.wait()

    def gather_z(k):
        return remote(pb.at[x, 0, y], pb.at[x, SLOT[k], y], az_s.at[k], az_r.at[k], at_z(k))

    for k in REL[1:]:
        gather_z(k).start()

    for s in range(NZ):

        def give(i, _, s=s):
            remote(
                frames.at[:, columns_of(s, i, 1 - c)],
                places_of(s, i),
                frame_sems.at[0],
                frame_sems.at[1],
                partner,
            ).start()
            return 0

        lax.fori_loop(0, NX, give, 0)
    mask_copy = remote(masks.at[c], masks.at[c], mask_sems.at[0], mask_sems.at[1], partner)
    mask_copy.start()

    def gather_xy(group, dx, dy):
        if group % 2 == 0:
            px, py = x, ys[-dy] if dx else y
            where = device(z, xs[dx], c, y) if dx else device(z, x, c, ys[dy])
        else:
            px, py = xs[-dx] if dy else x, y
            where = device(z, x, c, ys[dy]) if dy else device(z, xs[dx], c, y)
        piece = pb.at[px, group * PAIR : (group + 1) * PAIR, py]
        return remote(piece, piece, ap_s.at[group, dx, dy], ap_r.at[group, dx, dy], where)

    def leg(group, first, second):
        return gather_xy(group, *((second, first) if group % 2 == 0 else (first, second)))

    for group in range(GROUPS):
        for slot in range(max(1, group * PAIR), (group + 1) * PAIR):
            gather_z(REL[slot]).wait_recv()
        for d in ORDER:
            leg(group, d, 0).start()
        for d in ORDER:
            leg(group, 0, d).start()

    def turn(i, _):
        at = pl.ds(pl.multiple_of(i * BLOCK, BLOCK), BLOCK)
        block = w[:, at]
        wt[i // NZ, i % NZ] = block.T.reshape(NY, PIECE, 2 * count)
        moved = pltpu.roll(block.astype(jnp.float32), 1, 0)
        keep = masks[...].reshape(2 * count, BLOCK) > 0.5
        w[:, at] = jnp.where(keep, moved, 0.0).astype(jnp.bfloat16)
        return 0

    def forward(group, d):
        leg(group, d, 0).wait_recv()
        for e in ORDER:
            leg(group, d, e).start()

    for d in ORDER:
        forward(0, d)
        forward(1, d)
    mine_rows = w.at[pl.ds(pl.multiple_of(c * count, 128), count)]
    pltpu.make_async_copy(mine_rows, mine_rows, local_sem).wait()
    frames_copy = remote(mine_rows, mine_rows, frame_sems.at[0], frame_sems.at[1], partner)
    frames_copy.wait()
    mask_copy.wait()
    turned = 0
    for d, until in zip(ORDER, TURNS):
        lax.fori_loop(turned, until, turn, 0)
        turned = until
        forward(2, d)
        forward(3, d)
    lax.fori_loop(turned, NZ * NX, turn, 0)

    def swap(core):
        return remote(
            part.at[core], other.at[core], part_sems.at[0, core], part_sems.at[1, core], partner
        )

    depth = NZ * BLOCK
    for dx in (0,) + ORDER:
        for group in range(GROUPS):
            for dy in range(NY):
                if (dx if group % 2 == 0 else dy):
                    gather_xy(group, dx, dy).wait_recv()
        px = xs[-dx]
        block = pb[px].reshape(depth, pb.shape[-1])
        for core in range(NC):
            its = slice(core * count, (core + 1) * count)
            product = jnp.dot(
                w[its, pl.ds(pl.multiple_of(px * depth, depth), depth)],
                block,
                preferred_element_type=jnp.float32,
            )
            if dx == 0:
                part[core] = product
            else:
                part[core] += product
            if dx == ORDER[-1]:
                swap(core).start()
    for core in range(NC):
        swap(core).wait()
        paired[core * count : (core + 1) * count] = (part[core] + other[core]).astype(jnp.bfloat16)

    side = PAIR * PIECE

    def scatter_1(group, dx, dy):
        where = device(z, x, c, ys[dy]) if group % 2 else device(z, xs[dx], c, y)
        return remote(
            tsend.at[group, dx, dy],
            trecv.at[group, dx, dy],
            rs_s.at[group, dx, dy],
            rs_r.at[group, dx, dy],
            where,
        )

    def scatter_2(group, d):
        where = device(z, xs[d], c, y) if group % 2 else device(z, x, c, ys[d])
        return remote(
            tsend2.at[group, d], trecv2.at[group, d], rs2_s.at[group, d], rs2_r.at[group, d], where
        )

    def scatter_z(s):
        return remote(
            rows.at[s * PIECE : (s + 1) * PIECE],
            zrecv.at[s],
            rz_s.at[s],
            rz_r.at[s],
            at_z(NZ - REL[s]),
        )

    both = [(dx, dy) for dx in ORDER for dy in ORDER]
    both += [(d, 0) for d in ORDER] + [(0, d) for d in ORDER] + [(0, 0)]
    for groups in ((2, 3), (0, 1)):
        for dx, dy in both:
            slots = slice(groups[0] * PAIR, (groups[1] + 1) * PAIR)
            lhs = wt[xs[dx], slots, ys[dy]].reshape(2 * side, 2 * count)
            term = jnp.dot(lhs, paired[...], preferred_element_type=jnp.float32)
            for group, away, along in ((groups[0], dx, dy), (groups[1], dy, dx)):
                mine_term = term[(group % 2) * side : (group % 2 + 1) * side]
                if away:
                    tsend[group, dx, dy] = mine_term.astype(jnp.bfloat16)
                    scatter_1(group, dx, dy).start()
                else:
                    held[group, along] = mine_term

    def summed(group, along):
        total = held[group, along]
        for d in ORDER:
            at = (along, d) if group % 2 else (d, along)
            scatter_1(group, *at).wait_recv()
            total = total + trecv[group, at[0], at[1]].astype(jnp.float32)
        return total

    for groups in ((2, 3), (0, 1)):
        for d in ORDER:
            for group in groups:
                tsend2[group, d] = summed(group, d).astype(jnp.bfloat16)
                scatter_2(group, d).start()
    for groups in ((2, 3), (0, 1)):
        for group in groups:
            total = summed(group, 0)
            for d in ORDER:
                scatter_2(group, d).wait_recv()
                total = total + trecv2[group, d].astype(jnp.float32)
            rows[group * side : (group + 1) * side] = total
            for slot in reversed(range(max(1, group * PAIR), (group + 1) * PAIR)):
                scatter_z(slot).start()

    total = rows[:PIECE]
    for slot in reversed(range(1, NZ)):
        scatter_z(slot).wait_recv()
        total = total + zrecv[slot]
    total = total * scale
    here = pl.ds(pl.multiple_of(y * PIECE, PIECE), PIECE)
    sketch_ref[here] = total

    def gather_y(k):
        return remote(
            sketch_ref.at[here],
            sketch_ref.at[here],
            y_s.at[k],
            y_r.at[k],
            device(z, x, c, ys[k]),
        )

    gsend[...] = jnp.dot(
        total.T, total, preferred_element_type=jnp.float32, precision=lax.Precision.HIGHEST
    ).reshape(gsend.shape)

    def scatter_g(k):
        i = XYC_ORDER.index(k)
        return remote(gsend.at[place(k)], grecv.at[i], g_s.at[i], g_r.at[i], at_xyc(k))

    for k in XYC_ORDER:
        scatter_g(k).start()
    me = place((0, 0, 0))
    acc = gsend[me]
    for k in reversed(XYC_ORDER):
        scatter_g(k).wait_recv()
        acc = acc + grecv[XYC_ORDER.index(k)]
    gz[z] = acc

    def spread_z(k):
        return remote(gz.at[z], gz.at[z], gz_s.at[k], gz_r.at[k], at_z(k))

    for k in Z_ORDER:
        spread_z(k).start()
    for k in ORDER:
        gather_y(k).start()
    for k in Z_ORDER:
        spread_z(k).wait_recv()
    acc = gz[0]
    for k in range(1, NZ):
        acc = acc + gz[k]
    gram_ref[me] = acc

    def gather_g(k):
        i = XYC_ORDER.index(k)
        return remote(gram_ref.at[me], gram_ref.at[me], ga_s.at[i], ga_r.at[i], at_xyc(k))

    for k in XYC_ORDER:
        gather_g(k).start()

    for group in range(GROUPS):
        for dx in range(NX):
            for dy in range(NY):
                if dx or dy:
                    gather_xy(group, dx, dy).wait_send()
                if (dy if group % 2 else dx):
                    scatter_1(group, dx, dy).wait_send()
        for d in ORDER:
            scatter_2(group, d).wait_send()
    for k in Z_ORDER:
        gather_z(k).wait_send()
        scatter_z(k).wait_send()
        spread_z(k).wait_send()
    for k in XYC_ORDER:
        scatter_g(k).wait_send()
    for k in ORDER:
        gather_y(k).wait()
    for k in reversed(XYC_ORDER):
        gather_g(k).wait()


def sketch_and_gram(frames, lengths, probes, devices):
    count, width = frames.shape
    columns = probes.shape[1]
    scale = 1.0 / math.sqrt(width * count * devices)
    half = width // NC
    dma = pltpu.SemaphoreType.DMA
    f32, bf16 = jnp.float32, jnp.bfloat16
    return pl.pallas_call(
        functools.partial(kernel, scale),
        out_shape=(
            jax.ShapeDtypeStruct((BLOCK, columns), f32),
            jax.ShapeDtypeStruct((NXYC, columns // NXYC, columns), f32),
        ),
        in_specs=[
            pl.BlockSpec(memory_space=pltpu.HBM),
            pl.BlockSpec(memory_space=pltpu.HBM),
            pl.BlockSpec(memory_space=pltpu.HBM),
        ],
        out_specs=(pl.BlockSpec(memory_space=pltpu.VMEM), pl.BlockSpec(memory_space=pltpu.VMEM)),
        scratch_shapes=[
            pltpu.SMEM((1, 1, 4), jnp.int32),
            pltpu.VMEM((NC * count, half), bf16),
            pltpu.VMEM((NX, NZ, NY, PIECE, NC * count), bf16),
            pltpu.VMEM((NX, NZ, NY, PIECE, columns), bf16),
            pltpu.VMEM((NC, count, BLOCK), f32),
            pltpu.VMEM((NC, count, columns), f32),
            pltpu.VMEM((NC, count, columns), f32),
            pltpu.VMEM((NC * count, columns), bf16),
            pltpu.VMEM((GROUPS, NX, NY, PAIR * PIECE, columns), bf16),
            pltpu.VMEM((GROUPS, NX, NY, PAIR * PIECE, columns), bf16),
            pltpu.VMEM((GROUPS, NX, PAIR * PIECE, columns), bf16),
            pltpu.VMEM((GROUPS, NX, PAIR * PIECE, columns), bf16),
            pltpu.VMEM((GROUPS, NX, PAIR * PIECE, columns), f32),
            pltpu.VMEM((NZ * PIECE, columns), f32),
            pltpu.VMEM((NZ, PIECE, columns), f32),
            dma,
            dma,
            dma,
            dma((2,)),
            dma((2,)),
            dma((2, NC)),
            dma((NZ,)),
            dma((NZ,)),
            dma((GROUPS, NX, NY)),
            dma((GROUPS, NX, NY)),
            dma((GROUPS, NX, NY)),
            dma((GROUPS, NX, NY)),
            dma((GROUPS, NX)),
            dma((GROUPS, NX)),
            dma((NZ,)),
            dma((NZ,)),
            dma((NY,)),
            dma((NY,)),
            pltpu.VMEM((NXYC, columns // NXYC, columns), f32),
            pltpu.VMEM((NXYC, columns // NXYC, columns), f32),
            pltpu.VMEM((NZ, columns // NXYC, columns), f32),
            dma((NXYC,)),
            dma((NXYC,)),
            dma((NZ,)),
            dma((NZ,)),
            dma((NXYC,)),
            dma((NXYC,)),
        ],
        compiler_params=pltpu.CompilerParams(
            collective_id=0, has_side_effects=True, vmem_limit_bytes=48 << 20
        ),
    )(lengths, frames, probes)


LANES = 128
PANEL = 8


def splat(v):
    return lax.broadcast_in_dim(v, (PANEL, LANES), (0, 1))


def less(x, y, z):
    return lax.sub(x, lax.mul(y, z))


def finish_kernel(scale, sketch, gram, basis_out, factor_out, a, b, inverse, factor, basis, sems):
    n = gram.shape[0]
    panels = n // PANEL
    lane_tiles = n // LANES
    a[...] = gram[...]
    b[...] = jnp.where(
        lax.broadcasted_iota(jnp.int32, (n, n), 0) == lax.broadcasted_iota(jnp.int32, (n, n), 1),
        1.0,
        0.0,
    )

    def send(here, there, k):
        return pltpu.make_async_copy(here, there, sems.at[k])

    def tile(ref, top, rows, t):
        return ref.at[top : top + rows, t * LANES : (t + 1) * LANES]

    one = jnp.ones((PANEL, LANES), jnp.float32)
    for p in range(panels):
        top = p * PANEL
        first = top // LANES
        tiles = [(a, t) for t in range(first, lane_tiles)] + [(b, t) for t in range(first + 1)]
        many = range(len(tiles))
        d = [[splat(a[top + i : top + i + 1, top + j : top + j + 1]) for j in range(i + 1)] for i in range(PANEL)]
        rows = [[splat(tile(ref, top + i, 1, t)[...]) for ref, t in tiles] for i in range(PANEL)]
        m = [[None] * PANEL for _ in range(PANEL)]
        inv = [None] * PANEL
        for j in range(PANEL):
            inv[j] = lax.div(one, d[j][j])
            for i in range(j + 1, PANEL):
                m[i][j] = lax.mul(d[i][j], inv[j])
            for i in range(j + 1, PANEL):
                for k in range(j + 1, i + 1):
                    d[i][k] = less(d[i][k], m[i][j], d[k][j])
                for k in many:
                    rows[i][k] = less(rows[i][k], m[i][j], rows[j][k])
        w = [None] * PANEL
        for i in reversed(range(PANEL)):
            w[i] = []
            for k in many:
                acc = lax.mul(inv[i], rows[i][k])
                for q in reversed(range(i + 1, PANEL)):
                    acc = less(acc, m[q][i], w[q][k])
                w[i].append(acc)

        def update(below, _):
            here = pl.ds(pl.multiple_of(below * PANEL, PANEL), PANEL)
            v = [splat(a[here, top + j : top + j + 1]) for j in range(PANEL)]
            for k, (ref, t) in enumerate(tiles):
                block = ref.at[here, t * LANES : (t + 1) * LANES]
                value = block[...]
                for j in range(PANEL):
                    value = less(value, v[j], w[j][k])
                block[...] = value
            return 0

        last = (first + 1) * LANES // PANEL
        if p + 1 < last:
            lax.fori_loop(p + 1, last, update, 0, unroll=True)
        for i in range(PANEL):
            root = lax.rsqrt(d[i][i])
            for t in range(lane_tiles):
                upper = jnp.zeros((1, LANES), jnp.float32)
                lower = upper
                if t >= first:
                    upper = (rows[i][t - first] * root)[0:1]
                if t == first:
                    lane = lax.broadcasted_iota(jnp.int32, (1, LANES), 1) + t * LANES
                    upper = jnp.where(lane >= top + i, upper, 0.0)
                if t <= first:
                    lower = (rows[i][lane_tiles - first + t] * root)[0:1]
                tile(factor, top + i, 1, t)[...] = upper
                tile(inverse, top + i, 1, t)[...] = lower
        if p + 1 == last and last < panels:
            done, below = top + PANEL - LANES, top + PANEL
            right = factor[done:below, below:]
            taken = lax.dot_general(
                right,
                jnp.concatenate([inverse[done:below, :below], right], axis=1),
                (((0,), (0,)), ((), ())),
                precision=lax.Precision.HIGHEST,
                preferred_element_type=jnp.float32,
            )
            b[below:, :below] = b[below:, :below] - taken[:, :below]
            a[below:, below:] = a[below:, below:] - taken[:, below:]
        if p + 1 == last:
            send(factor.at[last * PANEL - LANES : last * PANEL], factor_out.at[last * PANEL - LANES : last * PANEL], 2 * first).start()
            basis[first] = scale * lax.dot_general(
                sketch[:, : last * PANEL],
                inverse[last * PANEL - LANES : last * PANEL, : last * PANEL],
                (((1,), (1,)), ((), ())),
                precision=lax.Precision.HIGHEST,
                preferred_element_type=jnp.float32,
            )
            send(basis.at[first], basis_out.at[:, last * PANEL - LANES : last * PANEL], 2 * first + 1).start()
    for t in range(lane_tiles):
        at = slice(t * LANES, (t + 1) * LANES)
        send(factor.at[at], factor_out.at[at], 2 * t).wait()
        send(basis.at[t], basis_out.at[:, at], 2 * t + 1).wait()


def finish(sketch, gram, scale):
    return pl.pallas_call(
        functools.partial(finish_kernel, scale),
        out_shape=(
            jax.ShapeDtypeStruct(sketch.shape, jnp.float32),
            jax.ShapeDtypeStruct(gram.shape, jnp.float32),
        ),
        in_specs=[pl.BlockSpec(memory_space=pltpu.VMEM)] * 2,
        out_specs=(pl.BlockSpec(memory_space=pltpu.HBM),) * 2,
        scratch_shapes=[pltpu.VMEM(gram.shape, jnp.float32)] * 4
        + [
            pltpu.VMEM((gram.shape[0] // LANES, sketch.shape[0], LANES), jnp.float32),
            pltpu.SemaphoreType.DMA((2 * gram.shape[0] // LANES,)),
        ],
        compiler_params=pltpu.CompilerParams(vmem_limit_bytes=32 << 20),
    )(sketch, gram)


def shards(frames, lengths, probes):
    local = frames.reshape(frames.shape[2], frames.shape[3])
    width = local.shape[1]
    columns = probes.shape[1]
    devices = lax.axis_size("dp") * lax.axis_size("group")
    lengths = pltpu.with_memory_space_constraint(lengths, pltpu.HBM)
    probes = pltpu.with_memory_space_constraint(probes, pltpu.HBM)
    sketch, gram = sketch_and_gram(local, lengths, probes, devices)
    gram = gram.reshape(columns, columns)
    return finish(sketch, gram, math.sqrt(width))


def solution(mesh):
    placed = (P("dp", "group", None, None), P("dp", "group", None), P("dp", None))
    return jax.shard_map(
        shards, mesh=mesh, in_specs=placed, out_specs=(P("dp", None), P()), check_vma=False
    )
```
